128 devices in a mesh: gx: 8 (over x, core), gy: 16 (over z, y).
Axes of the slice: x: 4, y: 4, z: 4, core: 2. Of those that a mesh axis runs over, the one named last changes fastest.
Arguments:
- rhs: bfloat16 [128, 262144], P(None, ('gx', 'gy')), may hold values from -6 to 6
- col_basis: bfloat16 [64, 262144], P(None, ('gx', 'gy')), may hold values from -0.375 to 0.375
- row_basis: bfloat16 [64, 262144], P(None, ('gx', 'gy')), may hold values from -0.75 to 0.75
- near_blocks: bfloat16 [4, 256, 262144], P(None, None, ('gx', 'gy')), may hold values from -0.1875 to 0.1875
- near_list: int32 [1024, 4], P(('gx', 'gy')), may hold values from 0 to 1023, as said below
- leaf_up: float32 [1024, 4096], P(('gx', 'gy')), may hold values from -0.5 to 0.5
- leaf_down: float32 [1024, 4096], P(('gx', 'gy')), may hold values from -0.75 to 0.75
- local_up: float32 [896, 4096], P(('gx', 'gy')), may hold values from -0.5 to 0.5
- local_down: float32 [896, 4096], P(('gx', 'gy')), may hold values from -0.75 to 0.75
- leaf_coupling: bfloat16 [1024, 64, 1024], P(('gx', 'gy')), may hold values from -0.1875 to 0.1875
- leaf_target: int32 [1024, 16], P(('gx', 'gy')), may hold values from 0 to 127, all different within a row; in each aligned block of 8 rows (0 to 7, 8 to 15, ...) at most 2 rows name the same one
- leaf_slot: int32 [1024, 16], P(('gx', 'gy')), may hold values from 0 to 7
- top_up: float32 [124, 4096], replicated, may hold values from -0.5 to 0.5
- top_down: float32 [124, 4096], replicated, may hold values from -0.75 to 0.75
- upper_coupling: bfloat16 [126, 4, 4096], replicated, may hold values from -0.375 to 0.375
- upper_partners: int32 [126, 4], replicated, may hold values from 0 to 63, as said below
Outputs:
- product: bfloat16 [128, 262144], P(None, ('gx', 'gy'))
The draws below stay inside these ranges and needn't reach their ends.
Inputs may be any that keep to these rules, and one draw needn't show every extreme that they name: `near_list`: row t begins with t itself; its other entries are leaves at most 8 away from t, clipped to the range; in each aligned block of 8 rows some entry lies exactly 8 above its row and some exactly 8 below it before clipping. `leaf_target`: each row names 16 different devices; among the rows of one device no device is named more than 2 times, and some device is named exactly 2 times. `upper_partners`: row row(m, i) names only clusters of level m other than i, by their index within level m.
All inputs are finite; a program needn't handle non-finite values.
Results may differ from the reference program's by a relative error of at most 0.0058.
Values may be sent and summed in bfloat16 or wider, within the bound.
A program may use at most 192 MiB of HBM per device.

```python
import math
import jax
import jax.numpy as jnp
import numpy as np
from jax import lax

K = 64
R = 128
P_SIZE = 256
LEAF_DEV = 8
NEAR = 4
FAR_LEAF = 16
FAR_TOP = 4
LEAVES = 1024
POINTS = 262144
LOCALS = 896
UPPERS = 126
TOPS = 124
CAP = 2
N_GX = 8
N_GY = 16


def draw_near_list(key, part):
    key = jax.random.fold_in(key, 11)
    key_shift, key_above, key_below = jax.random.split(key, 3)
    leaf_index = jnp.arange(LEAVES, dtype=jnp.int32)
    shifts = jax.random.randint(key_shift, (LEAVES, NEAR - 1), -LEAF_DEV, LEAF_DEV + 1, dtype=jnp.int32)
    owner = leaf_index // LEAF_DEV
    within = leaf_index % LEAF_DEV
    pick_above = jax.random.randint(key_above, (LEAVES // LEAF_DEV,), 0, LEAF_DEV, dtype=jnp.int32)
    pick_below = jax.random.randint(key_below, (LEAVES // LEAF_DEV,), 0, LEAF_DEV, dtype=jnp.int32)
    shifts = shifts.at[:, 0].set(jnp.where(within == pick_above[owner], LEAF_DEV, shifts[:, 0]))
    shifts = shifts.at[:, NEAR - 2].set(jnp.where(within == pick_below[owner], -LEAF_DEV, shifts[:, NEAR - 2]))
    neighbours = jnp.clip(leaf_index[:, None] + shifts, 0, LEAVES - 1)
    return jnp.concatenate([leaf_index[:, None], neighbours], axis=1).astype(jnp.int32)


def draw_upper_partners(key, part):
    key = jax.random.fold_in(key, 23)
    devices = N_GX * N_GY
    depth = devices.bit_length() - 1
    rows = jnp.arange(devices - 2, dtype=jnp.int32)
    count = jnp.zeros_like(rows) + 2
    place = jnp.zeros_like(rows)
    for level in range(1, depth):
        start = devices - (devices >> level - 1)
        level_size = devices >> level
        inside = (rows >= start) & (rows < start + level_size)
        count = jnp.where(inside, level_size, count)
        place = jnp.where(inside, rows - start, place)
    shifts = jax.random.randint(key, (devices - 2, FAR_TOP), 1, count[:, None], dtype=jnp.int32)
    shifts = shifts.at[0, 0].set(devices // 2 - 1).at[1, 0].set(devices // 2 - 1)
    return ((place[:, None] + shifts) % count[:, None]).astype(jnp.int32)


def with_ends(values, key, smallest, high):
    longest = values.shape.index(max(values.shape))
    spots = []
    for shift in (0, 1):
        where = [jax.random.randint(jax.random.fold_in(key, axis), (), 0, length) for axis, length in enumerate(values.shape)]
        where[longest] = (where[longest] + shift) % values.shape[longest]
        spots.append(tuple(where))
    return values.at[spots[0]].set(smallest).at[spots[1]].set(high)


def steps_of(own_key, dims, cuts, low, largest):
    factor_of = 1.0
    for dim, blocks in cuts:
        steps = jax.random.uniform(jax.random.fold_in(jax.random.fold_in(own_key, 6), dim), (blocks,), jnp.float32, low / len(cuts), largest / len(cuts))
        factor_of = factor_of * jnp.repeat(jnp.exp(steps), dims[dim] // blocks).reshape((-1,) + (1,) * (len(dims) - 1 - dim))
    return factor_of


def routed_block(stream_key, own, number, rows, number_of, top, most, lean):
    ranking = jax.random.permutation(stream_key, number_of)
    packed, ordinary = portions_of(number_of, rows * top, most, lean, True), portions_of(number_of, rows * top, most, lean, False)
    places = jnp.arange(number_of)

    def named(tallies, turn):
        used = int((tallies > 0).sum())
        fixed = max(1, used // 4)
        passed = fixed + (places - fixed + turn * (used - fixed)) % max(1, number_of - fixed)
        return jnp.zeros((number_of,), jnp.int32).at[ranking[jnp.where(places < fixed, places, passed)]].set(jnp.asarray(tallies, jnp.int32))

    tallies = jnp.where(number % 4 == 0, named(packed, number // 4), named(ordinary, number - number // 4 - 1))
    mixed = jax.random.permutation(jax.random.fold_in(own, 3), number_of)
    giver, receiver = mixed[0:number_of // 2 * 2:2], mixed[1:number_of // 2 * 2:2]
    slack = jnp.minimum(tallies[giver] - 1, most - tallies[receiver]) // 2
    slack = jnp.where((giver == ranking[0]) | (receiver == ranking[0]) | (tallies[receiver] == 0), 0, jnp.maximum(slack, 0))
    passed = jax.random.randint(jax.random.fold_in(own, 4), (number_of // 2,), 0, 1 << 20) % (slack + 1)
    tallies = tallies.at[giver].add(-passed).at[receiver].add(passed)
    labels = jnp.searchsorted(jnp.cumsum(tallies), jnp.arange(rows * top), side="right").astype(jnp.int32)
    listing = labels.reshape(top, rows).T
    listing = listing[jax.random.permutation(jax.random.fold_in(own, 1), rows)]
    turn = jax.random.randint(jax.random.fold_in(own, 2), (rows, 1), 0, top)
    return jnp.take_along_axis(listing, (jnp.arange(top)[None, :] + turn) % top, axis=1)


def portions_of(number_of, total, most, slope, full):
    loads = [(1 << 20) // math.isqrt(standing ** slope) + 1 for standing in range(1, number_of + 1)]
    largest = most if full else min(most, max(-(-total // number_of), total * loads[0] // sum(loads)))
    least = 1 if total - largest >= number_of - 1 else 0
    given, surplus = [largest] + [least] * (number_of - 1), total - largest - least * (number_of - 1)
    while surplus > 0:
        candidates = [i for i in range(1, number_of) if given[i] < largest] or [i for i in range(1, number_of) if given[i] < most]
        pool, budget = sum([loads[i] for i in candidates]), surplus
        for i in candidates:
            more = min(most - given[i], max(1, budget * loads[i] // pool), surplus)
            given[i] = given[i] + more
            surplus = surplus - more
    return np.array(given)


def noise(key, dims, deviation, reach, cuts=(), held_as=jnp.bfloat16):
    gain = steps_of(key, dims, cuts, -0.22, 0.18) if cuts else 1.0
    entries = jax.random.normal(key, dims, jnp.float32) * deviation * gain
    return jnp.minimum(jnp.maximum(entries, -reach), reach).astype(held_as)


def setup_inputs(seed: int = 0) -> dict:
    splits = jax.random.split(jax.random.key(seed), 17)
    rhs = noise(splits[0], (R, POINTS), 1.0, 6.0, ((1, 128),))
    col_basis = noise(splits[1], (K, POINTS), P_SIZE ** -0.5, 0.375, ((1, 128),))
    row_basis = noise(splits[2], (K, POINTS), K ** -0.5, 0.75, ((1, 128),))
    near_blocks = noise(splits[3], (NEAR, P_SIZE, POINTS), (P_SIZE * NEAR) ** -0.5, 0.1875, ((2, 128),))
    near_list = draw_near_list(jax.random.fold_in(splits[16], 71), 0)
    leaf_up = noise(splits[5], (LEAVES, K * K), (2 * K) ** -0.5, 0.5, ((0, 128),), jnp.float32)
    leaf_down = noise(splits[6], (LEAVES, K * K), K ** -0.5, 0.75, ((0, 128),), jnp.float32)
    local_up = noise(splits[7], (LOCALS, K * K), (2 * K) ** -0.5, 0.5, ((0, 128),), jnp.float32)
    local_down = noise(splits[8], (LOCALS, K * K), K ** -0.5, 0.75, ((0, 128),), jnp.float32)
    leaf_coupling = noise(splits[9], (LEAVES, K, FAR_LEAF * K), (K * FAR_LEAF) ** -0.5, 0.1875, ((0, 128),))
    leaf_target_keys = jax.random.split(jax.random.fold_in(splits[10], 1), LEAVES // LEAF_DEV)
    leaf_target_turns = jax.random.permutation(jax.random.fold_in(splits[10], 3), LEAVES // LEAF_DEV)
    leaf_target = jax.vmap(lambda own, number: routed_block(jax.random.fold_in(splits[10], 2), own, number, LEAF_DEV, N_GX * N_GY, FAR_LEAF, CAP, 2))(leaf_target_keys, leaf_target_turns).reshape((LEAVES, FAR_LEAF))
    leaf_slot = with_ends(jax.random.randint(splits[11], (LEAVES, FAR_LEAF), 0, LEAF_DEV), jax.random.fold_in(splits[11], 1), 0, LEAF_DEV - 1).astype(jnp.int32)
    top_up = noise(splits[12], (TOPS, K * K), (2 * K) ** -0.5, 0.5, (), jnp.float32)
    top_down = noise(splits[13], (TOPS, K * K), K ** -0.5, 0.75, (), jnp.float32)
    upper_coupling = noise(splits[14], (UPPERS, FAR_TOP, K * K), (K * FAR_TOP) ** -0.5, 0.375)
    upper_partners = draw_upper_partners(jax.random.fold_in(splits[16], 71), 0)
    return {"rhs": rhs, "col_basis": col_basis, "row_basis": row_basis, "near_blocks": near_blocks, "near_list": near_list, "leaf_up": leaf_up, "leaf_down": leaf_down, "local_up": local_up, "local_down": local_down, "leaf_coupling": leaf_coupling, "leaf_target": leaf_target, "leaf_slot": leaf_slot, "top_up": top_up, "top_down": top_down, "upper_coupling": upper_coupling, "upper_partners": upper_partners}


PRECISE = lax.Precision.HIGHEST


def rounded(value):
    return lax.optimization_barrier(value.astype(jnp.bfloat16)).astype(jnp.float32)


def apply_blocks(coef, blocks):
    return jnp.einsum('...rk,...km->...rm', coef, blocks, precision=PRECISE)


def reference(rhs, col_basis, row_basis, near_blocks, near_list, leaf_up, leaf_down, local_up, local_down, leaf_coupling, leaf_target, leaf_slot, top_up, top_down, upper_coupling, upper_partners):
    devices = N_GX * N_GY
    depth_top = devices.bit_length() - 1
    rhs_blocks = rhs.reshape(R, LEAVES, P_SIZE).astype(jnp.float32)
    basis_col = col_basis.reshape(K, LEAVES, P_SIZE).astype(jnp.float32)
    leaf_coef = jnp.einsum('rlp,klp->lrk', rhs_blocks, basis_col, precision=PRECISE)
    coef_low = rounded(leaf_coef)

    def couple(pieces):
        coef_part, coupling_part = pieces
        blocks = coupling_part.reshape(LEAF_DEV, K, FAR_LEAF, K).astype(jnp.float32)
        return jnp.einsum('lrk,lkjm->ljrm', coef_part, blocks, precision=PRECISE).astype(jnp.bfloat16)

    products = lax.map(couple, (coef_low.reshape(devices, LEAF_DEV, R, K), leaf_coupling.reshape(devices, LEAF_DEV, K, FAR_LEAF * K)))
    target = (leaf_target * LEAF_DEV + leaf_slot).reshape(-1)
    leaf_far = jnp.zeros((LEAVES, R, K), jnp.float32).at[target].add(products.reshape(-1, R, K).astype(jnp.float32))

    lifted = apply_blocks(leaf_coef, leaf_up.reshape(LEAVES, K, K))
    coef = (lifted[0::2] + lifted[1::2]).reshape(devices, LEAF_DEV // 2, R, K)
    local_ups = local_up.reshape(devices, LEAF_DEV - 1, K, K)
    start = 0
    count = LEAF_DEV // 2
    while count > 1:
        lifted = apply_blocks(coef, local_ups[:, start:start + count])
        coef = lifted[:, 0::2] + lifted[:, 1::2]
        start += count
        count //= 2
    root_lift = apply_blocks(coef[:, 0], local_ups[:, start])

    top_ups = top_up.reshape(devices - 4, K, K)
    upper_levels = [root_lift[0::2] + root_lift[1::2]]
    for level in range(2, depth_top):
        count = devices >> (level - 1)
        start = devices - (devices >> (level - 2))
        lifted = apply_blocks(upper_levels[-1], top_ups[start:start + count])
        upper_levels.append(lifted[0::2] + lifted[1::2])

    couplings = upper_coupling.reshape(devices - 2, FAR_TOP, K, K).astype(jnp.float32)
    upper_far = []
    for level in range(1, depth_top):
        count = devices >> level
        start = devices - (devices >> (level - 1))
        upper_low = rounded(upper_levels[level - 1])
        sources = upper_low[upper_partners[start:start + count]]
        upper_far.append(jnp.einsum('cjrk,cjkm->crm', sources, couplings[start:start + count], precision=PRECISE))

    top_downs = top_down.reshape(devices - 4, K, K)
    answer = upper_far[-1]
    for level in range(depth_top - 2, 0, -1):
        count = devices >> level
        start = devices - (devices >> (level - 1))
        answer = upper_far[level - 1] + apply_blocks(jnp.repeat(answer, 2, axis=0), top_downs[start:start + count])
    local_downs = local_down.reshape(devices, LEAF_DEV - 1, K, K)
    answer = apply_blocks(jnp.repeat(answer, 2, axis=0), local_downs[:, LEAF_DEV - 2])[:, None]
    count = 2
    while count < LEAF_DEV:
        start = LEAF_DEV - 2 * count
        answer = apply_blocks(jnp.repeat(answer, 2, axis=1), local_downs[:, start:start + count])
        count *= 2
    parents = jnp.repeat(answer.reshape(LEAVES // 2, R, K), 2, axis=0)
    leaf_answer = leaf_far + apply_blocks(parents, leaf_down.reshape(LEAVES, K, K))
    answer_low = rounded(leaf_answer)
    basis_row = row_basis.reshape(K, LEAVES, P_SIZE).astype(jnp.float32)
    far_out = jnp.einsum('lrk,klp->rlp', answer_low, basis_row, precision=PRECISE)

    def near_part(device):
        rows = lax.dynamic_slice_in_dim(near_list, device * LEAF_DEV, LEAF_DEV, 0)
        sources = jnp.take(rhs_blocks, rows, axis=1)
        blocks = lax.dynamic_slice_in_dim(near_blocks, device * (LEAF_DEV * P_SIZE), LEAF_DEV * P_SIZE, 2)
        blocks = blocks.reshape(NEAR, P_SIZE, LEAF_DEV, P_SIZE).astype(jnp.float32)
        return jnp.einsum('rljq,jqlp->rlp', sources, blocks, precision=PRECISE)

    near = lax.map(near_part, jnp.arange(devices, dtype=jnp.int32))
    near = jnp.transpose(near, (1, 0, 2, 3)).reshape(R, LEAVES, P_SIZE)
    return (far_out + near).astype(jnp.bfloat16).reshape(R, POINTS)
```

```python
import jax
import jax.numpy as jnp
from jax import lax
from jax.experimental import pallas as pl
from jax.experimental.pallas import tpu as pltpu
from jax.sharding import PartitionSpec as P

K = 64
R = 128
P_SIZE = 256
LEAF_DEV = 8
NEAR = 4
FAR_LEAF = 16
FAR_TOP = 4
NX = 8
NY = 16
D = NX * NY
HALF = K // 2
MESH = pl.DeviceIdType.MESH
BF = jnp.bfloat16
F32 = jnp.float32


def mm(a, b):
    return jnp.dot(a, b, preferred_element_type=F32)


def split(x):
    hi = x.astype(BF)
    return hi, (x - hi.astype(F32)).astype(BF)


def precise(a, w):
    a_hi, a_lo = split(a)
    w_hi, w_lo = split(w)
    return mm(a_hi, w_hi) + (mm(a_lo, w_hi) + mm(a_hi, w_lo))


def unroll(rows, count, squares, first):
    for q in range(K // 2):
        pair = rows[:, q * 2 * K:(q + 1) * 2 * K].astype(F32)
        for h in range(2):
            at = first * K + 2 * q + h
            squares[pl.ds(at, count, stride=K), :] = pair[:, h * K:(h + 1) * K]


def kernel(
    src_sm, near_sm, part_sm,
    rhs, col, leaf_up, leaf_down, local_up, local_down, code_a, code_b,
    row_hbm, near_hbm, coup_hbm, tup_hbm, tdn_hbm, ucp_hbm,
    out,
    rhs3, nearv, coupv, rowv, tupv, tdnv, ucpv,
    prods, send_a, recv_a, send_b, recv_b, meta_a, meta_b, codes_a, codes_b,
    send_a2, recv_a2, send_b2, recv_b2,
    roots, tiles_hi, tiles_lo, tops, squares, near_acc, tree_leaf,
    local_sem, send_sem, recv_sem,
):
    mx = lax.axis_index("gx")
    my = lax.axis_index("gy")
    me = mx * NY + my

    def fetch(src, dst, number):
        copy = pltpu.make_async_copy(src, dst, local_sem.at[number])
        copy.start()
        return copy

    def remote(src, dst, number, device):
        pltpu.make_async_remote_copy(
            src_ref=src, dst_ref=dst, send_sem=send_sem.at[number], recv_sem=recv_sem.at[number],
            device_id=device, device_id_type=MESH,
        ).start()

    def finish(ref, sem):
        pltpu.make_async_copy(ref, ref, sem).wait()

    def block(i):
        return squares[i * K:(i + 1) * K, :]

    def peers_x():
        return [lax.rem(mx + i, NX) for i in range(1, NX)]

    def peers_y():
        return [lax.rem(my + i, NY) for i in range(1, NY)]

    nxt = lax.rem(me + 1, D)
    prv = lax.rem(me + D - 1, D)
    sides = ((lax.div(nxt, NY), lax.rem(nxt, NY)), (lax.div(prv, NY), lax.rem(prv, NY)))

    barrier = pltpu.get_barrier_semaphore()
    for x in peers_x():
        pl.semaphore_signal(barrier, inc=1, device_id=(x, my), device_id_type=MESH)
    for y in peers_y():
        pl.semaphore_signal(barrier, inc=1, device_id=(mx, y), device_id_type=MESH)
    for side in sides:
        pl.semaphore_signal(barrier, inc=1, device_id=side, device_id_type=MESH)

    got_coup = fetch(coup_hbm, coupv, 0)
    got_near = fetch(near_hbm, nearv, 1)
    got_row = fetch(row_hbm, rowv, 2)
    got_tup = fetch(tup_hbm, tupv, 3)
    got_tdn = fetch(tdn_hbm, tdnv, 4)
    rows_up = [D - (D >> level - 1) + lax.div(me, 1 << level) for level in range(1, 7)]
    got_ucp = [fetch(ucp_hbm.at[rows_up[m]], ucpv.at[m], 5 + m) for m in range(6)]

    def part(ref, l):
        return ref[:, l * P_SIZE:(l + 1) * P_SIZE]

    nt = (((1,), (1,)), ((), ()))
    tn = (((0,), (0,)), ((), ()))
    low = [
        lax.dot_general(part(col, l), part(rhs, l), nt, preferred_element_type=F32).astype(BF)
        for l in range(LEAF_DEV)
    ]

    for l in range(LEAF_DEV):
        rhs3[LEAF_DEV + l] = part(rhs, l)
    own = rhs3.at[pl.ds(LEAF_DEV, LEAF_DEV)]
    pl.semaphore_wait(barrier, NX + NY)
    for j, side in enumerate(sides):
        remote(own, rhs3.at[pl.ds(2 * j * LEAF_DEV, LEAF_DEV)], j, side)
    for x in peers_x():
        remote(code_a.at[x], meta_a.at[mx], 2, (x, my))
    for y in peers_y():
        remote(code_b.at[y], meta_b.at[my], 3, (mx, y))
    meta_a[mx] = code_a[mx]
    meta_b[my] = code_b[my]

    got_coup.wait()
    for l in range(LEAF_DEV):
        product = lax.dot_general(coupv[l], low[l], tn, preferred_element_type=F32)
        prods[l * FAR_LEAF:(l + 1) * FAR_LEAF] = product.astype(BF).reshape(FAR_LEAF, K, R)

    def place_b(y):
        for x in range(NX):
            for c in range(2):
                product = prods[src_sm[(x * NY + y) * 2 + c]]
                send_b[y, x, c * HALF:(c + 1) * HALF, :] = product[HALF:]

    def step_b(i, _):
        y = lax.rem(my + i, NY)
        place_b(y)
        remote(send_b.at[y], recv_b.at[:, my], 4, (mx, y))
        return 0

    def place_a(x):
        for y in range(NY):
            for c in range(2):
                product = prods[src_sm[(x * NY + y) * 2 + c]]
                send_a[x, y, c * HALF:(c + 1) * HALF, :] = product[:HALF]

    def step_a(i, _):
        x = lax.rem(mx + i, NX)
        place_a(x)
        remote(send_a.at[x], recv_a.at[:, mx], 5, (x, my))
        return 0

    lax.fori_loop(1, NY, step_b, 0)
    lax.fori_loop(1, NX, step_a, 0)
    place_b(my)
    place_a(mx)
    recv_b[:, my] = send_b[my]
    recv_a[:, mx] = send_a[mx]

    coef = [
        lax.dot_general(part(rhs, l), part(col, l), nt, preferred_element_type=F32)
        for l in range(LEAF_DEV)
    ]
    unroll(leaf_up, 8, squares, 0)
    lifted = [precise(coef[l], block(l)) for l in range(LEAF_DEV)]
    unroll(local_up, 7, squares, 8)
    start = 8
    while len(lifted) > 1:
        coef = [lifted[2 * i] + lifted[2 * i + 1] for i in range(len(lifted) // 2)]
        lifted = [
            precise(coef[i], block(start + i)) for i in range(len(coef))
        ]
        start += len(coef)
    roots[my] = jnp.concatenate(split(lifted[0]), axis=1)
    for y in peers_y():
        remote(roots.at[my], roots.at[my], 6, (mx, y))

    got_near.wait()
    for l in range(LEAF_DEV):
        near_acc[:, l * P_SIZE:(l + 1) * P_SIZE] = mm(part(rhs, l), nearv[0, :, l * P_SIZE:(l + 1) * P_SIZE])

    finish(roots.at[pl.ds(0, NY - 1)], recv_sem.at[6])
    first_lanes = lax.broadcasted_iota(jnp.int32, (R, 2 * K), 1) < K
    for i in range(4):
        r = [roots[4 * i + h].astype(F32) for h in range(4)]
        r = [r[0] + r[1], r[2] + r[3]]
        r = [v + pltpu.roll(v, K, 1) for v in r]
        tiles_hi[mx * 4 + i] = jnp.where(first_lanes, r[0], r[1]).astype(BF)
    for x in peers_x():
        remote(tiles_hi.at[pl.ds(mx * 4, 4)], tiles_hi.at[pl.ds(mx * 4, 4)], 7, (x, my))

    for j in range(2):
        finish(own, recv_sem.at[j])
    for l in range(LEAF_DEV):
        total = near_acc[:, l * P_SIZE:(l + 1) * P_SIZE]
        for j in range(1, NEAR):
            source = rhs3[near_sm[l * NEAR + j]]
            total += mm(source, nearv[j, :, l * P_SIZE:(l + 1) * P_SIZE])
        near_acc[:, l * P_SIZE:(l + 1) * P_SIZE] = total

    got_tup.wait()

    def turn(g, _):
        unroll(tupv.at[pl.ds(g * 8, 8)], 8, tops, g * 8)
        return 0

    lax.fori_loop(0, 15, turn, 0)
    unroll(tupv.at[120:124], 4, tops, 120)
    unroll(local_down, 7, squares, 15)
    unroll(leaf_down, 8, squares, 22)
    got_tdn.wait()
    for m in range(5):
        unroll(tdnv.at[pl.ds(rows_up[m], 1)], 1, squares, 30 + m)
    for m in range(6):
        got_ucp[m].wait()
        unroll(ucpv.at[m], FAR_TOP, squares, 35 + m * FAR_TOP)

    finish(meta_a.at[pl.ds(0, NX - 1)], recv_sem.at[2])
    finish(meta_b.at[pl.ds(0, NY - 1)], recv_sem.at[3])
    lanes = lax.broadcasted_iota(jnp.int32, (NY, 128), 1) < 2 * HALF
    for q in range(NX // 2):
        codes_a[:, q * 128:(q + 1) * 128] = jnp.where(lanes, meta_a[2 * q], meta_a[2 * q + 1])
    lanes = lax.broadcasted_iota(jnp.int32, (NX, 128), 1) < 2 * HALF
    for q in range(NY // 2):
        codes_b[:, q * 128:(q + 1) * 128] = jnp.where(lanes, meta_b[2 * q], meta_b[2 * q + 1])

    def gathered(codes, recv, g):
        width = codes.shape[1]
        rows = lax.broadcasted_iota(jnp.int32, (LEAF_DEV * HALF, width), 0)
        hits = jnp.where(rows == codes[pl.ds(g, 1), :], 1.0, 0.0).astype(BF)
        return mm(hits, recv[g].reshape(width, R)).astype(BF)

    finish(recv_a.at[:, pl.ds(0, NX - 1)], recv_sem.at[5])

    def sum_a(i, _):
        y = lax.rem(my + i, NY)
        send_a2[y] = gathered(codes_a, recv_a, y)
        remote(send_a2.at[y], recv_a2.at[my], 8, (mx, y))
        return 0

    lax.fori_loop(1, NY, sum_a, 0)
    recv_a2[my] = gathered(codes_a, recv_a, my)
    finish(recv_b.at[:, pl.ds(0, NY - 1)], recv_sem.at[4])

    def sum_b(i, _):
        x = lax.rem(mx + i, NX)
        send_b2[x] = gathered(codes_b, recv_b, x)
        remote(send_b2.at[x], recv_b2.at[mx], 9, (x, my))
        return 0

    lax.fori_loop(1, NX, sum_b, 0)
    recv_b2[mx] = gathered(codes_b, recv_b, mx)

    finish(tiles_hi.at[pl.ds(0, 28)], recv_sem.at[7])

    def merge(t, _):
        halves = []
        for h in range(2):
            tile = 2 * t + h
            a = tiles_hi[tile]
            wh, wl = split(tops[pl.ds(tile * 2 * K, 2 * K), :])
            halves.append((a, wh, wl, tile))
        return halves

    def merge_first(t, _):
        merged = [mm(a, wh) + mm(a, wl) for a, wh, wl, _ in merge(t, None)]
        hi, lo = split(jnp.concatenate(merged, axis=1))
        tiles_hi[32 + t] = hi
        tiles_lo[t] = lo
        return 0

    def merge_next(t, _):
        merged = [
            mm(a, wh) + (mm(a, wl) + mm(tiles_lo[tile - 32], wh)) for a, wh, wl, tile in merge(t, None)
        ]
        hi, lo = split(jnp.concatenate(merged, axis=1))
        tiles_hi[32 + t] = hi
        tiles_lo[t] = lo
        return 0

    lax.fori_loop(0, 16, merge_first, 0)
    lax.fori_loop(16, 31, merge_next, 0)

    fars = []
    for m in range(6):
        total = None
        for j in range(FAR_TOP):
            partner = part_sm[rows_up[m] * FAR_TOP + j]
            tile = tiles_hi[64 - (64 >> m) + lax.div(partner, 2)].astype(F32)
            side = jnp.full((R, K), lax.rem(partner, 2), jnp.int32)
            picked = jnp.where(side == 0, tile[:, :K], tile[:, K:])
            term = mm(picked.astype(BF), block(35 + m * FAR_TOP + j).astype(BF))
            total = term if total is None else total + term
        fars.append(total)
    answer = fars[5]
    for m in range(4, -1, -1):
        answer = fars[m] + precise(answer, block(30 + m))
    answers = [precise(answer, block(15 + 6))]
    for count in (2, 4):
        start = 15 + LEAF_DEV - 2 * count
        answers = [precise(answers[i // 2], block(start + i)) for i in range(count)]
    for l in range(LEAF_DEV):
        tree_leaf[l] = precise(answers[l // 2], block(22 + l)).T

    got_row.wait()
    finish(recv_a2.at[pl.ds(0, NY - 1)], recv_sem.at[8])
    finish(recv_b2.at[pl.ds(0, NX - 1)], recv_sem.at[9])
    for l in range(LEAF_DEV):
        upper = recv_a2[0, l * HALF:(l + 1) * HALF, :].astype(F32)
        for s in range(1, NY):
            upper += recv_a2[s, l * HALF:(l + 1) * HALF, :].astype(F32)
        lower = recv_b2[0, l * HALF:(l + 1) * HALF, :].astype(F32)
        for s in range(1, NX):
            lower += recv_b2[s, l * HALF:(l + 1) * HALF, :].astype(F32)
        answer_low = (jnp.concatenate([upper, lower], axis=0) + tree_leaf[l]).astype(BF)
        far = lax.dot_general(answer_low, part(rowv, l), tn, preferred_element_type=F32)
        out[:, l * P_SIZE:(l + 1) * P_SIZE] = (far + part(near_acc, l)).astype(BF)

    for j in range(2):
        finish(own, send_sem.at[j])
    finish(meta_a.at[pl.ds(0, NX - 1)], send_sem.at[2])
    finish(meta_b.at[pl.ds(0, NY - 1)], send_sem.at[3])
    finish(send_b.at[pl.ds(0, NY - 1)], send_sem.at[4])
    finish(send_a.at[pl.ds(0, NX - 1)], send_sem.at[5])
    finish(roots.at[pl.ds(0, NY - 1)], send_sem.at[6])
    finish(tiles_hi.at[pl.ds(0, 28)], send_sem.at[7])
    finish(send_a2.at[pl.ds(0, NY - 1)], send_sem.at[8])
    finish(send_b2.at[pl.ds(0, NX - 1)], send_sem.at[9])


def body(
    rhs, col_basis, row_basis, near_blocks, near_list, leaf_up, leaf_down, local_up, local_down,
    leaf_coupling, leaf_target, leaf_slot, top_up, top_down, upper_coupling, upper_partners,
):
    total = LEAF_DEV * FAR_LEAF
    target = leaf_target.reshape(total)
    order = jnp.arange(total, dtype=jnp.int32)
    earlier = (target[:, None] == target[None, :]) & (order[None, :] < order[:, None])
    placed = 2 * target + jnp.sum(earlier.astype(jnp.int32), axis=1)
    matches = placed[None, :] == jnp.arange(2 * D, dtype=jnp.int32)[:, None]
    source = jnp.max(jnp.where(matches, order[None, :], 0), axis=1)
    slots = jnp.max(jnp.where(matches, leaf_slot.reshape(total)[None, :], -1), axis=1)
    slots = slots.reshape(NX, NY, 1, 2, 1)
    code = jnp.where(slots >= 0, slots * HALF + jnp.arange(HALF, dtype=jnp.int32), -1)
    code_a = jnp.broadcast_to(code, (NX, NY, 2, 2, HALF)).reshape(NX, NY, 4 * HALF)
    code_b = jnp.swapaxes(code_a, 0, 1)
    device = lax.axis_index("gx") * NY + lax.axis_index("gy")
    near = near_list.reshape(-1) - (device * LEAF_DEV - LEAF_DEV)
    smem = pl.BlockSpec(memory_space=pltpu.SMEM)
    vmem = pl.BlockSpec(memory_space=pltpu.VMEM)
    hbm = pl.BlockSpec(memory_space=pl.ANY)
    width = LEAF_DEV * P_SIZE
    return pl.pallas_call(
        kernel,
        out_shape=jax.ShapeDtypeStruct((R, width), BF),
        in_specs=[smem] * 3 + [vmem] * 8 + [hbm] * 6,
        out_specs=vmem,
        scratch_shapes=[
            pltpu.VMEM((3 * LEAF_DEV, R, P_SIZE), BF),
            pltpu.VMEM((NEAR, P_SIZE, width), BF),
            pltpu.VMEM((LEAF_DEV, K, FAR_LEAF * K), BF),
            pltpu.VMEM((K, width), BF),
            pltpu.VMEM((D - 4, K * K), F32),
            pltpu.VMEM((D - 4, K * K), F32),
            pltpu.VMEM((6, FAR_TOP, K * K), BF),
            pltpu.VMEM((total, K, R), BF),
            pltpu.VMEM((NX, NY, K, R), BF),
            pltpu.VMEM((NY, NX, K, R), BF),
            pltpu.VMEM((NY, NX, K, R), BF),
            pltpu.VMEM((NX, NY, K, R), BF),
            pltpu.VMEM((NX, NY, 128), jnp.int32),
            pltpu.VMEM((NY, NX, 128), jnp.int32),
            pltpu.VMEM((NY, NX * K), jnp.int32),
            pltpu.VMEM((NX, NY * K), jnp.int32),
            pltpu.VMEM((NY, LEAF_DEV * HALF, R), BF),
            pltpu.VMEM((NY, LEAF_DEV * HALF, R), BF),
            pltpu.VMEM((NX, LEAF_DEV * HALF, R), BF),
            pltpu.VMEM((NX, LEAF_DEV * HALF, R), BF),
            pltpu.VMEM((NY, R, 2 * K), BF),
            pltpu.VMEM((63, R, 2 * K), BF),
            pltpu.VMEM((31, R, 2 * K), BF),
            pltpu.VMEM(((D - 4) * K, K), F32),
            pltpu.VMEM((59 * K, K), F32),
            pltpu.VMEM((R, width), F32),
            pltpu.VMEM((LEAF_DEV, K, R), F32),
            pltpu.SemaphoreType.DMA((11,)),
            pltpu.SemaphoreType.DMA((10,)),
            pltpu.SemaphoreType.DMA((10,)),
        ],
        compiler_params=pltpu.CompilerParams(
            collective_id=0, has_side_effects=True, vmem_limit_bytes=60 * 1024 * 1024
        ),
    )(
        source, near, upper_partners.reshape(-1),
        rhs, col_basis, leaf_up, leaf_down, local_up, local_down, code_a, code_b,
        row_basis, near_blocks, leaf_coupling, top_up, top_down, upper_coupling,
    )


def solution(mesh):
    flat = ("gx", "gy")
    placed = (
        P(None, flat), P(None, flat), P(None, flat), P(None, None, flat),
        P(flat, None), P(flat, None), P(flat, None), P(flat, None), P(flat, None),
        P(flat, None, None), P(flat, None), P(flat, None),
        P(), P(), P(), P(),
    )
    return jax.shard_map(body, mesh=mesh, in_specs=placed, out_specs=P(None, flat), check_vma=False)
```

```python
import jax
import jax.numpy as jnp
from jax import lax
from jax.experimental import pallas as pl
from jax.experimental.pallas import tpu as pltpu
from jax.sharding import PartitionSpec as P

K = 64
R = 128
P_SIZE = 256
LEAF_DEV = 8
NEAR = 4
FAR_LEAF = 16
FAR_TOP = 4
NX = 8
NY = 16
D = NX * NY
HALF = K // 2
MESH = pl.DeviceIdType.MESH
BF = jnp.bfloat16
F32 = jnp.float32


def mm(a, b):
    return jnp.dot(a, b, preferred_element_type=F32)


def split(x):
    hi = x.astype(BF)
    return hi, (x - hi.astype(F32)).astype(BF)


def precise(a, w):
    a_hi, a_lo = split(a)
    w_hi, w_lo = split(w)
    return mm(a_hi, w_hi) + (mm(a_lo, w_hi) + mm(a_hi, w_lo))


def unroll(rows, count, squares, first):
    for q in range(K // 2):
        pair = rows[:, q * 2 * K:(q + 1) * 2 * K].astype(F32)
        for h in range(2):
            at = first * K + 2 * q + h
            squares[pl.ds(at, count, stride=K), :] = pair[:, h * K:(h + 1) * K]


def kernel(
    near_sm, part_sm,
    rhs, col, leaf_up, leaf_down, local_up, local_down, target, slot,
    row_hbm, near_hbm, coup_hbm, tup_hbm, tdn_hbm, ucp_hbm,
    out,
    rhs3, nearv, coupv, rowv, tupv, tdnv, ucpv,
    table, table_sm, code, code_b,
    prods, send_a, recv_a, send_b, recv_b, meta_a, meta_b, codes_a, codes_b,
    send_a2, recv_a2, send_b2, recv_b2, send_a3, recv_a3, send_b3, recv_b3,
    roots, tiles_hi, tiles_lo, tops, squares, near_acc, tree_leaf,
    local_sem, send_sem, recv_sem,
):
    mx = lax.axis_index("gx")
    my = lax.axis_index("gy")
    me = mx * NY + my
    cx, cc = lax.div(mx, 2), lax.rem(mx, 2)
    cz, cy = lax.div(my, 4), lax.rem(my, 4)
    zc = cz * 2 + cc

    def at_x(x):
        return (x * 2 + cc, my)

    def at_y(y):
        return (mx, cz * 4 + y)

    def at_z(z):
        return (mx, z * 4 + cy)

    def at_gx(x):
        return (x, my)

    def at_zc(g):
        return (cx * 2 + lax.rem(g, 2), lax.div(g, 2) * 4 + cy)

    sibling = (cx * 2 + 1 - cc, my)

    def fetch(src, dst, number):
        copy = pltpu.make_async_copy(src, dst, local_sem.at[number])
        copy.start()
        return copy

    def remote(src, dst, number, device):
        pltpu.make_async_remote_copy(
            src_ref=src, dst_ref=dst, send_sem=send_sem.at[number], recv_sem=recv_sem.at[number],
            device_id=device, device_id_type=MESH,
        ).start()

    def finish(ref, sem):
        pltpu.make_async_copy(ref, ref, sem).wait()

    def block(i):
        return squares[i * K:(i + 1) * K, :]

    def others(mine, count):
        return [lax.rem(mine + i, count) for i in range(1, count)]

    nxt = lax.rem(me + 1, D)
    prv = lax.rem(me + D - 1, D)
    sides = ((lax.div(nxt, NY), lax.rem(nxt, NY)), (lax.div(prv, NY), lax.rem(prv, NY)))

    barrier = pltpu.get_barrier_semaphore()
    peers = [at_gx(x) for x in others(mx, NX)] + [at_zc(g) for g in others(zc, 8)]
    peers += [at_y(y) for y in others(cy, 4)] + list(sides)
    for peer in peers:
        pl.semaphore_signal(barrier, inc=1, device_id=peer, device_id_type=MESH)

    got_coup = fetch(coup_hbm, coupv, 0)
    got_near = fetch(near_hbm, nearv, 1)
    got_row = fetch(row_hbm, rowv, 2)
    got_tup = fetch(tup_hbm, tupv, 3)
    got_tdn = fetch(tdn_hbm, tdnv, 4)
    rows_up = [D - (D >> level - 1) + lax.div(me, 1 << level) for level in range(1, 7)]
    got_ucp = [fetch(ucp_hbm.at[rows_up[m]], ucpv.at[m], 5 + m) for m in range(6)]

    lane = lax.broadcasted_iota(jnp.int32, (LEAF_DEV, D), 1)
    row = lax.broadcasted_iota(jnp.int32, (LEAF_DEV, D), 0)
    named = jnp.full((LEAF_DEV, D), -1, jnp.int32)
    for j in range(FAR_LEAF):
        entry = (row * FAR_LEAF + j) * LEAF_DEV + slot[:, j:j + 1]
        named = jnp.where(target[:, j:j + 1] == lane, entry, named)
    last = jnp.max(named, axis=0, keepdims=True)
    first = jnp.min(jnp.where(named < 0, 1 << 20, named), axis=0, keepdims=True)
    first = jnp.where(last < 0, -1, first)
    last = jnp.where(last == first, -1, last)
    lists = jnp.where(row == 0, first, last)
    table[...] = lax.shift_right_logical(jnp.maximum(lists, 0), 3)
    got_table = fetch(table, table_sm, 11)

    def part(ref, l):
        return ref[:, l * P_SIZE:(l + 1) * P_SIZE]

    nt = (((1,), (1,)), ((), ()))
    tn = (((0,), (0,)), ((), ()))
    low = [
        lax.dot_general(part(col, l), part(rhs, l), nt, preferred_element_type=F32).astype(BF)
        for l in range(LEAF_DEV)
    ]
    for l in range(LEAF_DEV):
        rhs3[LEAF_DEV + l] = part(rhs, l)
    own = rhs3.at[pl.ds(LEAF_DEV, LEAF_DEV)]
    wide = lax.broadcasted_iota(jnp.int32, (D, D), 1)
    pick = jnp.where(
        (wide & HALF) == 0,
        jnp.broadcast_to(first, (D, D)).T,
        jnp.broadcast_to(last, (D, D)).T,
    )
    code[...] = jnp.where(pick < 0, -1, (pick & (LEAF_DEV - 1)) * HALF + (wide & (HALF - 1)))
    for g in range(8):
        for y in range(4):
            base = (g % 2) * NY + (g // 2) * 4 + y
            code_b[g, y * 4:(y + 1) * 4, :] = code[pl.ds(base, 4, stride=2 * NY), :]

    pl.semaphore_wait(barrier, len(peers))
    for j, side in enumerate(sides):
        remote(own, rhs3.at[pl.ds(2 * j * LEAF_DEV, LEAF_DEV)], j, side)
    for x in others(mx, NX):
        remote(code.at[pl.ds(pl.multiple_of(x * NY, NY), NY)], meta_a.at[mx], 2, at_gx(x))
    for g in others(zc, 8):
        remote(code_b.at[g], meta_b.at[zc], 3, at_zc(g))
    meta_a[mx] = code[pl.ds(pl.multiple_of(mx * NY, NY), NY), :]
    meta_b[zc] = code_b[zc]

    got_coup.wait()
    for l in range(LEAF_DEV):
        product = lax.dot_general(coupv[l], low[l], tn, preferred_element_type=F32)
        prods[l * FAR_LEAF:(l + 1) * FAR_LEAF] = product.astype(BF).reshape(FAR_LEAF, K, R)

    got_table.wait()

    def place_a(x):
        for g in range(NY):
            for c in range(2):
                product = prods[table_sm[c, x * NY + g]]
                send_a[x, g, c * HALF:(c + 1) * HALF, :] = product[:HALF]

    def place_b(g):
        for y in range(4):
            for x in range(4):
                device = (x * 2 + lax.rem(g, 2)) * NY + lax.div(g, 2) * 4 + y
                for c in range(2):
                    product = prods[table_sm[c, device]]
                    send_b[g, y * 4 + x, c * HALF:(c + 1) * HALF, :] = product[HALF:]

    def step_first(i, _):
        x = lax.rem(mx + i, NX)
        place_a(x)
        remote(send_a.at[x], recv_a.at[:, mx], 5, at_gx(x))
        g = lax.rem(zc + i, 8)
        place_b(g)
        remote(send_b.at[g], recv_b.at[:, zc], 4, at_zc(g))
        return 0

    lax.fori_loop(1, NX, step_first, 0)
    place_a(mx)
    place_b(zc)
    recv_a[:, mx] = send_a[mx]
    recv_b[:, zc] = send_b[zc]

    coef = [
        lax.dot_general(part(rhs, l), part(col, l), nt, preferred_element_type=F32)
        for l in range(LEAF_DEV)
    ]
    unroll(leaf_up, 8, squares, 0)
    lifted = [precise(coef[l], block(l)) for l in range(LEAF_DEV)]
    unroll(local_up, 7, squares, 8)
    start = 8
    while len(lifted) > 1:
        coef = [lifted[2 * i] + lifted[2 * i + 1] for i in range(len(lifted) // 2)]
        lifted = [precise(coef[i], block(start + i)) for i in range(len(coef))]
        start += len(coef)
    roots[cy] = jnp.concatenate(split(lifted[0]), axis=1)
    for y in others(cy, 4):
        remote(roots.at[cy], roots.at[cy], 6, at_y(y))

    got_near.wait()
    for l in range(LEAF_DEV):
        near_acc[:, l * P_SIZE:(l + 1) * P_SIZE] = mm(part(rhs, l), nearv[0, :, l * P_SIZE:(l + 1) * P_SIZE])

    finish(roots.at[pl.ds(0, 3)], recv_sem.at[6])
    first_lanes = lax.broadcasted_iota(jnp.int32, (R, 2 * K), 1) < K
    r = [roots[h].astype(F32) for h in range(4)]
    r = [r[0] + r[1], r[2] + r[3]]
    r = [v + pltpu.roll(v, K, 1) for v in r]
    mine = tiles_hi.at[mx * 4 + cz]
    mine[...] = jnp.where(first_lanes, r[0], r[1]).astype(BF)
    for z in others(cz, 4):
        remote(mine, mine, 7, at_z(z))

    for j in range(2):
        finish(own, recv_sem.at[j])
    for l in range(LEAF_DEV):
        total = near_acc[:, l * P_SIZE:(l + 1) * P_SIZE]
        for j in range(1, NEAR):
            at = near_sm[l, j] - (me * LEAF_DEV - LEAF_DEV)
            source = rhs3[jnp.minimum(jnp.maximum(at, 0), 3 * LEAF_DEV - 1)]
            total += mm(source, nearv[j, :, l * P_SIZE:(l + 1) * P_SIZE])
        near_acc[:, l * P_SIZE:(l + 1) * P_SIZE] = total

    got_tup.wait()

    def turn(g, _):
        unroll(tupv.at[pl.ds(g * 8, 8)], 8, tops, g * 8)
        return 0

    lax.fori_loop(0, 15, turn, 0)
    unroll(tupv.at[120:124], 4, tops, 120)
    unroll(local_down, 7, squares, 15)
    unroll(leaf_down, 8, squares, 22)
    got_tdn.wait()
    for m in range(5):
        unroll(tdnv.at[pl.ds(rows_up[m], 1)], 1, squares, 30 + m)
    for m in range(6):
        got_ucp[m].wait()
        unroll(ucpv.at[m], FAR_TOP, squares, 35 + m * FAR_TOP)

    finish(tiles_hi.at[pl.ds(0, 3)], recv_sem.at[7])
    plane = tiles_hi.at[pl.ds(mx * 4, 4)]
    for x in others(cx, 4):
        remote(plane, plane, 10, at_x(x))

    finish(meta_a.at[pl.ds(0, 7)], recv_sem.at[2])
    finish(meta_b.at[pl.ds(0, 7)], recv_sem.at[3])
    lanes = lax.broadcasted_iota(jnp.int32, (NY, 128), 1) < 2 * HALF
    for q in range(NX // 2):
        codes_a[:, q * 128:(q + 1) * 128] = jnp.where(lanes, meta_a[2 * q], meta_a[2 * q + 1])
        codes_b[:, q * 128:(q + 1) * 128] = jnp.where(lanes, meta_b[2 * q], meta_b[2 * q + 1])

    def gathered(codes, recv, g):
        width = codes.shape[1]
        rows = lax.broadcasted_iota(jnp.int32, (LEAF_DEV * HALF, width), 0)
        hits = jnp.where(rows == codes[pl.ds(g, 1), :], 1.0, 0.0).astype(BF)
        return mm(hits, recv[g].reshape(width, R)).astype(BF)

    finish(recv_a.at[:, pl.ds(0, 7)], recv_sem.at[5])

    def sum_a(i, _):
        z = lax.rem(cz + i, 4)
        for y in range(4):
            send_a2[z, y] = gathered(codes_a, recv_a, z * 4 + y)
        remote(send_a2.at[z], recv_a2.at[cz], 8, at_z(z))
        return 0

    lax.fori_loop(1, 4, sum_a, 0)
    for y in range(4):
        recv_a2[cz, y] = gathered(codes_a, recv_a, cz * 4 + y)
    finish(recv_b.at[:, pl.ds(0, 7)], recv_sem.at[4])

    def sum_b(i, _):
        y = lax.rem(cy + i, 4)
        for x in range(4):
            send_b2[y, x] = gathered(codes_b, recv_b, y * 4 + x)
        remote(send_b2.at[y], recv_b2.at[cy], 9, at_y(y))
        return 0

    lax.fori_loop(1, 4, sum_b, 0)
    for x in range(4):
        recv_b2[cy, x] = gathered(codes_b, recv_b, cy * 4 + x)

    finish(tiles_hi.at[pl.ds(0, 12)], recv_sem.at[10])
    for x in range(4):
        half = tiles_hi.at[pl.ds((x * 2 + cc) * 4, 4)]
        remote(half, half, 11, sibling)

    finish(tiles_hi.at[pl.ds(0, 16)], recv_sem.at[11])

    def merge(t):
        halves = []
        for h in range(2):
            tile = 2 * t + h
            wh, wl = split(tops[pl.ds(tile * 2 * K, 2 * K), :])
            halves.append((tiles_hi[tile], wh, wl, tile))
        return halves

    def keep(t, merged):
        hi, lo = split(jnp.concatenate(merged, axis=1))
        tiles_hi[32 + t] = hi
        tiles_lo[t] = lo
        return 0

    def merge_first(t, _):
        return keep(t, [mm(a, wh) + mm(a, wl) for a, wh, wl, _ in merge(t)])

    def merge_next(t, _):
        return keep(t, [
            mm(a, wh) + (mm(a, wl) + mm(tiles_lo[tile - 32], wh)) for a, wh, wl, tile in merge(t)
        ])

    for t in range(31):
        if t < 16:
            merge_first(t, 0)
        else:
            merge_next(t, 0)

    def summed(recv, place):
        total = recv[0, place].astype(F32)
        for s in range(1, 4):
            total += recv[s, place].astype(F32)
        return total.astype(BF)

    finish(recv_a2.at[pl.ds(0, 3)], recv_sem.at[8])
    for y in others(cy, 4):
        send_a3[y] = summed(recv_a2, y)
        remote(send_a3.at[y], recv_a3.at[cy], 12, at_y(y))
    recv_a3[cy] = summed(recv_a2, cy)
    finish(recv_b2.at[pl.ds(0, 3)], recv_sem.at[9])
    for x in others(cx, 4):
        send_b3[x] = summed(recv_b2, x)
        remote(send_b3.at[x], recv_b3.at[cx], 13, at_x(x))
    recv_b3[cx] = summed(recv_b2, cx)

    fars = []
    for m in range(6):
        total = None
        for j in range(FAR_TOP):
            partner = part_sm[rows_up[m], j]
            tile = tiles_hi[64 - (64 >> m) + lax.div(partner, 2)].astype(F32)
            side = jnp.full((R, K), lax.rem(partner, 2), jnp.int32)
            picked = jnp.where(side == 0, tile[:, :K], tile[:, K:])
            term = mm(picked.astype(BF), block(35 + m * FAR_TOP + j).astype(BF))
            total = term if total is None else total + term
        fars.append(total)
    answer = fars[5]
    for m in range(4, -1, -1):
        answer = fars[m] + precise(answer, block(30 + m))
    answers = [precise(answer, block(15 + 6))]
    for count in (2, 4):
        start = 15 + LEAF_DEV - 2 * count
        answers = [precise(answers[i // 2], block(start + i)) for i in range(count)]
    for l in range(LEAF_DEV):
        tree_leaf[l] = precise(answers[l // 2], block(22 + l)).T

    got_row.wait()
    finish(recv_a3.at[pl.ds(0, 3)], recv_sem.at[12])
    finish(recv_b3.at[pl.ds(0, 3)], recv_sem.at[13])
    for l in range(LEAF_DEV):
        rows = slice(l * HALF, (l + 1) * HALF)
        upper = recv_a3[0, rows, :].astype(F32)
        lower = recv_b3[0, rows, :].astype(F32)
        for s in range(1, 4):
            upper += recv_a3[s, rows, :].astype(F32)
            lower += recv_b3[s, rows, :].astype(F32)
        answer_low = (jnp.concatenate([upper, lower], axis=0) + tree_leaf[l]).astype(BF)
        far = lax.dot_general(answer_low, part(rowv, l), tn, preferred_element_type=F32)
        out[:, l * P_SIZE:(l + 1) * P_SIZE] = (far + part(near_acc, l)).astype(BF)

    for j in range(2):
        finish(own, send_sem.at[j])
    finish(meta_a.at[pl.ds(0, 7)], send_sem.at[2])
    finish(meta_b.at[pl.ds(0, 7)], send_sem.at[3])
    finish(send_b.at[pl.ds(0, 7)], send_sem.at[4])
    finish(send_a.at[pl.ds(0, 7)], send_sem.at[5])
    finish(roots.at[pl.ds(0, 3)], send_sem.at[6])
    finish(tiles_hi.at[pl.ds(0, 3)], send_sem.at[7])
    finish(send_a2.at[pl.ds(0, 3)], send_sem.at[8])
    finish(send_b2.at[pl.ds(0, 3)], send_sem.at[9])
    finish(tiles_hi.at[pl.ds(0, 12)], send_sem.at[10])
    finish(tiles_hi.at[pl.ds(0, 16)], send_sem.at[11])
    finish(send_a3.at[pl.ds(0, 3)], send_sem.at[12])
    finish(send_b3.at[pl.ds(0, 3)], send_sem.at[13])


def body(
    rhs, col_basis, row_basis, near_blocks, near_list, leaf_up, leaf_down, local_up, local_down,
    leaf_coupling, leaf_target, leaf_slot, top_up, top_down, upper_coupling, upper_partners,
):
    smem = pl.BlockSpec(memory_space=pltpu.SMEM)
    vmem = pl.BlockSpec(memory_space=pltpu.VMEM)
    hbm = pl.BlockSpec(memory_space=pl.ANY)
    width = LEAF_DEV * P_SIZE
    leaf_rows = LEAF_DEV * HALF
    return pl.pallas_call(
        kernel,
        out_shape=jax.ShapeDtypeStruct((R, width), BF),
        in_specs=[smem] * 2 + [vmem] * 8 + [hbm] * 6,
        out_specs=vmem,
        scratch_shapes=[
            pltpu.VMEM((3 * LEAF_DEV, R, P_SIZE), BF),
            pltpu.VMEM((NEAR, P_SIZE, width), BF),
            pltpu.VMEM((LEAF_DEV, K, FAR_LEAF * K), BF),
            pltpu.VMEM((K, width), BF),
            pltpu.VMEM((D - 4, K * K), F32),
            pltpu.VMEM((D - 4, K * K), F32),
            pltpu.VMEM((6, FAR_TOP, K * K), BF),
            pltpu.VMEM((8, D), jnp.int32),
            pltpu.SMEM((8, D), jnp.int32),
            pltpu.VMEM((D, D), jnp.int32),
            pltpu.VMEM((8, NY, D), jnp.int32),
            pltpu.VMEM((LEAF_DEV * FAR_LEAF, K, R), BF),
            pltpu.VMEM((8, NY, K, R), BF),
            pltpu.VMEM((NY, 8, K, R), BF),
            pltpu.VMEM((8, NY, K, R), BF),
            pltpu.VMEM((NY, 8, K, R), BF),
            pltpu.VMEM((8, NY, D), jnp.int32),
            pltpu.VMEM((8, NY, D), jnp.int32),
            pltpu.VMEM((NY, 8 * K), jnp.int32),
            pltpu.VMEM((NY, 8 * K), jnp.int32),
            pltpu.VMEM((4, 4, leaf_rows, R), BF),
            pltpu.VMEM((4, 4, leaf_rows, R), BF),
            pltpu.VMEM((4, 4, leaf_rows, R), BF),
            pltpu.VMEM((4, 4, leaf_rows, R), BF),
            pltpu.VMEM((4, leaf_rows, R), BF),
            pltpu.VMEM((4, leaf_rows, R), BF),
            pltpu.VMEM((4, leaf_rows, R), BF),
            pltpu.VMEM((4, leaf_rows, R), BF),
            pltpu.VMEM((4, R, 2 * K), BF),
            pltpu.VMEM((63, R, 2 * K), BF),
            pltpu.VMEM((31, R, 2 * K), BF),
            pltpu.VMEM(((D - 4) * K, K), F32),
            pltpu.VMEM((59 * K, K), F32),
            pltpu.VMEM((R, width), F32),
            pltpu.VMEM((LEAF_DEV, K, R), F32),
            pltpu.SemaphoreType.DMA((12,)),
            pltpu.SemaphoreType.DMA((14,)),
            pltpu.SemaphoreType.DMA((14,)),
        ],
        compiler_params=pltpu.CompilerParams(
            collective_id=0, has_side_effects=True, vmem_limit_bytes=60 * 1024 * 1024
        ),
    )(
        near_list, upper_partners,
        rhs, col_basis, leaf_up, leaf_down, local_up, local_down, leaf_target, leaf_slot,
        row_basis, near_blocks, leaf_coupling, top_up, top_down, upper_coupling,
    )


def solution(mesh):
    flat = ("gx", "gy")
    placed = (
        P(None, flat), P(None, flat), P(None, flat), P(None, None, flat),
        P(flat, None), P(flat, None), P(flat, None), P(flat, None), P(flat, None),
        P(flat, None, None), P(flat, None), P(flat, None),
        P(), P(), P(), P(),
    )
    return jax.shard_map(body, mesh=mesh, in_specs=placed, out_specs=P(None, flat), check_vma=False)
```

```python
import jax
import jax.numpy as jnp
from jax import lax
from jax.experimental import pallas as pl
from jax.experimental.pallas import tpu as pltpu
from jax.sharding import PartitionSpec as P

K = 64
R = 128
P_SIZE = 256
LEAF_DEV = 8
NEAR = 4
FAR_LEAF = 16
FAR_TOP = 4
NX = 8
NY = 16
D = NX * NY
HALF = K // 2
MESH = pl.DeviceIdType.MESH
BF = jnp.bfloat16
F32 = jnp.float32


def mm(a, b):
    return jnp.dot(a, b, preferred_element_type=F32)


def split(x):
    hi = x.astype(BF)
    return hi, (x - hi.astype(F32)).astype(BF)


def precise(a, w):
    a_hi, a_lo = split(a)
    w_hi, w_lo = split(w)
    return mm(a_hi, w_hi) + (mm(a_lo, w_hi) + mm(a_hi, w_lo))


def unroll(rows, count, squares, first):
    for q in range(K // 2):
        pair = rows[:, q * 2 * K:(q + 1) * 2 * K].astype(F32)
        for h in range(2):
            at = first * K + 2 * q + h
            squares[pl.ds(at, count, stride=K), :] = pair[:, h * K:(h + 1) * K]


def kernel(
    near_sm, part_sm,
    rhs, col, leaf_up, leaf_down, local_up, local_down, target, slot,
    row_hbm, near_hbm, coup_hbm, tup_hbm, tdn_hbm, ucp_hbm,
    out,
    rhs3, wrapped, nearv, coupv, rowv, tupv, tdnv, ucpv,
    table, table_sm, code, code_b,
    prods, send_a, recv_a, send_b, recv_b, meta_a, meta_b, codes_a, codes_b,
    send_a2, recv_a2, send_b2, recv_b2, send_a3, recv_a3, send_b3, recv_b3,
    roots, tiles_hi, tiles_lo, tops, squares, near_acc, tree_leaf,
    local_sem, send_sem, recv_sem,
):
    mx = lax.axis_index("gx")
    my = lax.axis_index("gy")
    me = mx * NY + my
    cx, cc = lax.div(mx, 2), lax.rem(mx, 2)
    cz, cy = lax.div(my, 4), lax.rem(my, 4)
    zc = cz * 2 + cc

    def at_x(x):
        return (x * 2 + cc, my)

    def at_y(y):
        return (mx, cz * 4 + y)

    def at_z(z):
        return (mx, z * 4 + cy)

    def at_gx(x):
        return (x, my)

    def at_zc(g):
        return (cx * 2 + lax.rem(g, 2), lax.div(g, 2) * 4 + cy)

    sibling = (cx * 2 + 1 - cc, my)

    def fetch(src, dst, number):
        copy = pltpu.make_async_copy(src, dst, local_sem.at[number])
        copy.start()
        return copy

    def remote(src, dst, number, device):
        pltpu.make_async_remote_copy(
            src_ref=src, dst_ref=dst, send_sem=send_sem.at[number], recv_sem=recv_sem.at[number],
            device_id=device, device_id_type=MESH,
        ).start()

    def finish(ref, sem):
        pltpu.make_async_copy(ref, ref, sem).wait()

    def block(i):
        return squares[i * K:(i + 1) * K, :]

    def others(mine, count):
        return [lax.rem(mine + i, count) for i in range(1, count)]

    above = lax.rem(me + 4, D)
    below = lax.rem(me + D - 4, D)
    above = (lax.div(above, NY), lax.rem(above, NY))
    below = (lax.div(below, NY), lax.rem(below, NY))

    barrier = pltpu.get_barrier_semaphore()
    peers = [at_gx(x) for x in others(mx, NX)] + [at_zc(g) for g in others(zc, 8)]
    peers += [at_y(y) for y in others(cy, 4)] + [above, below]
    for peer in peers:
        pl.semaphore_signal(barrier, inc=1, device_id=peer, device_id_type=MESH)

    got_coup = fetch(coup_hbm, coupv, 0)
    got_near = fetch(near_hbm, nearv, 1)
    got_row = fetch(row_hbm, rowv, 2)
    got_tup = fetch(tup_hbm, tupv, 3)
    got_tdn = fetch(tdn_hbm, tdnv, 4)
    rows_up = [D - (D >> level - 1) + lax.div(me, 1 << level) for level in range(1, 7)]
    got_ucp = [fetch(ucp_hbm.at[rows_up[m]], ucpv.at[m], 5 + m) for m in range(6)]

    lane = lax.broadcasted_iota(jnp.int32, (LEAF_DEV, D), 1)
    row = lax.broadcasted_iota(jnp.int32, (LEAF_DEV, D), 0)
    named = jnp.full((LEAF_DEV, D), -1, jnp.int32)
    for j in range(FAR_LEAF):
        entry = (row * FAR_LEAF + j) * LEAF_DEV + slot[:, j:j + 1]
        named = jnp.where(target[:, j:j + 1] == lane, entry, named)
    last = jnp.max(named, axis=0, keepdims=True)
    first = jnp.min(jnp.where(named < 0, 1 << 20, named), axis=0, keepdims=True)
    first = jnp.where(last < 0, -1, first)
    last = jnp.where(last == first, -1, last)
    lists = jnp.where(row == 0, first, last)
    table[...] = lax.shift_right_logical(jnp.maximum(lists, 0), 3)
    got_table = fetch(table, table_sm, 11)

    def part(ref, l):
        return ref[:, l * P_SIZE:(l + 1) * P_SIZE]

    nt = (((1,), (1,)), ((), ()))
    tn = (((0,), (0,)), ((), ()))
    low = [
        lax.dot_general(part(col, l), part(rhs, l), nt, preferred_element_type=F32).astype(BF)
        for l in range(LEAF_DEV)
    ]
    for l in range(LEAF_DEV):
        rhs3[LEAF_DEV + l] = part(rhs, l)
    own = rhs3.at[pl.ds(LEAF_DEV, LEAF_DEV)]
    wide = lax.broadcasted_iota(jnp.int32, (D, D), 1)
    pick = jnp.where(
        (wide & HALF) == 0,
        jnp.broadcast_to(first, (D, D)).T,
        jnp.broadcast_to(last, (D, D)).T,
    )
    code[...] = jnp.where(pick < 0, -1, (pick & (LEAF_DEV - 1)) * HALF + (wide & (HALF - 1)))
    for g in range(8):
        for x in range(4):
            base = (x * 2 + g % 2) * NY + (g // 2) * 4
            code_b[g, x * 4:(x + 1) * 4, :] = code[base:base + 4, :]

    meta_a[mx] = code[pl.ds(pl.multiple_of(mx * NY, NY), NY), :]
    meta_b[zc] = code_b[zc]

    got_coup.wait()
    for l in range(LEAF_DEV):
        product = lax.dot_general(coupv[l], low[l], tn, preferred_element_type=F32)
        prods[l * FAR_LEAF:(l + 1) * FAR_LEAF] = product.astype(BF).reshape(FAR_LEAF, K, R)

    got_table.wait()
    pl.semaphore_wait(barrier, len(peers))
    before = rhs3.at[pl.ds(0, LEAF_DEV)]
    after = rhs3.at[pl.ds(2 * LEAF_DEV, LEAF_DEV)]
    up, down = at_y(lax.rem(cy + 1, 4)), at_y(lax.rem(cy + 3, 4))
    starts, ends = cy == 0, cy == 3

    @pl.when(ends)
    def _():
        remote(own, wrapped, 15, up)
        remote(own, after, 1, down)

    @pl.when(starts)
    def _():
        remote(own, before, 0, up)
        remote(own, wrapped, 15, down)

    @pl.when(jnp.logical_and(cy > 0, cy < 3))
    def _():
        remote(own, before, 0, up)
        remote(own, after, 1, down)

    for x in others(mx, NX):
        remote(code.at[pl.ds(pl.multiple_of(x * NY, NY), NY)], meta_a.at[mx], 2, at_gx(x))
    for g in others(zc, 8):
        remote(code_b.at[g], meta_b.at[zc], 3, at_zc(g))

    def place_a(x):
        for g in range(NY):
            for c in range(2):
                product = prods[table_sm[c, x * NY + g]]
                send_a[x, g, c * HALF:(c + 1) * HALF, :] = product[:HALF]

    def place_b(g):
        for x in range(4):
            for y in range(4):
                device = (x * 2 + lax.rem(g, 2)) * NY + lax.div(g, 2) * 4 + y
                for c in range(2):
                    product = prods[table_sm[c, device]]
                    send_b[g, x * 4 + y, c * HALF:(c + 1) * HALF, :] = product[HALF:]

    def step_first(i, _):
        x = lax.rem(mx + i, NX)
        place_a(x)
        remote(send_a.at[x], recv_a.at[:, mx], 5, at_gx(x))
        g = lax.rem(zc + i, 8)
        place_b(g)
        remote(send_b.at[g], recv_b.at[:, zc], 4, at_zc(g))
        return 0

    lax.fori_loop(1, NX, step_first, 0)
    place_a(mx)
    place_b(zc)
    recv_a[:, mx] = send_a[mx]
    recv_b[:, zc] = send_b[zc]

    coef = [
        lax.dot_general(part(rhs, l), part(col, l), nt, preferred_element_type=F32)
        for l in range(LEAF_DEV)
    ]
    unroll(leaf_up, 8, squares, 0)
    lifted = [precise(coef[l], block(l)) for l in range(LEAF_DEV)]
    unroll(local_up, 7, squares, 8)
    start = 8
    while len(lifted) > 1:
        coef = [lifted[2 * i] + lifted[2 * i + 1] for i in range(len(lifted) // 2)]
        lifted = [precise(coef[i], block(start + i)) for i in range(len(coef))]
        start += len(coef)
    roots[cy] = jnp.concatenate(split(lifted[0]), axis=1)
    for y in others(cy, 4):
        remote(roots.at[cy], roots.at[cy], 6, at_y(y))

    got_near.wait()
    for l in range(LEAF_DEV):
        near_acc[:, l * P_SIZE:(l + 1) * P_SIZE] = mm(part(rhs, l), nearv[0, :, l * P_SIZE:(l + 1) * P_SIZE])

    finish(roots.at[pl.ds(0, 3)], recv_sem.at[6])
    first_lanes = lax.broadcasted_iota(jnp.int32, (R, 2 * K), 1) < K
    r = [roots[h].astype(F32) for h in range(4)]
    r = [r[0] + r[1], r[2] + r[3]]
    r = [v + pltpu.roll(v, K, 1) for v in r]
    mine = tiles_hi.at[mx * 4 + cz]
    mine[...] = jnp.where(first_lanes, r[0], r[1]).astype(BF)
    for z in others(cz, 4):
        remote(mine, mine, 7, at_z(z))

    got_tup.wait()

    def turn(g, _):
        unroll(tupv.at[pl.ds(g * 8, 8)], 8, tops, g * 8)
        return 0

    lax.fori_loop(0, 15, turn, 0)
    unroll(tupv.at[120:124], 4, tops, 120)
    unroll(local_down, 7, squares, 15)
    unroll(leaf_down, 8, squares, 22)
    got_tdn.wait()
    for m in range(5):
        unroll(tdnv.at[pl.ds(rows_up[m], 1)], 1, squares, 30 + m)
    for m in range(6):
        got_ucp[m].wait()
        unroll(ucpv.at[m], FAR_TOP, squares, 35 + m * FAR_TOP)

    finish(tiles_hi.at[pl.ds(0, 3)], recv_sem.at[7])
    column = tiles_hi.at[mx * 4 + cy]
    for x in others(cx, 4):
        remote(column, column, 10, at_x(x))

    finish(tiles_hi.at[pl.ds(0, 3)], recv_sem.at[10])
    for x in others(cx, 4):
        column = tiles_hi.at[(x * 2 + cc) * 4 + cy]
        for y in others(cy, 4):
            remote(column, column, 14, at_y(y))
    finish(meta_a.at[pl.ds(0, 7)], recv_sem.at[2])
    finish(meta_b.at[pl.ds(0, 7)], recv_sem.at[3])
    lanes = lax.broadcasted_iota(jnp.int32, (NY, 128), 1) < 2 * HALF
    for q in range(NX // 2):
        codes_a[:, q * 128:(q + 1) * 128] = jnp.where(lanes, meta_a[2 * q], meta_a[2 * q + 1])
        codes_b[:, q * 128:(q + 1) * 128] = jnp.where(lanes, meta_b[2 * q], meta_b[2 * q + 1])

    def gathered(codes, recv, g):
        width = codes.shape[1]
        rows = lax.broadcasted_iota(jnp.int32, (LEAF_DEV * HALF, width), 0)
        hits = jnp.where(rows == codes[pl.ds(g, 1), :], 1.0, 0.0).astype(BF)
        return mm(hits, recv[g].reshape(width, R)).astype(BF)

    finish(recv_a.at[:, pl.ds(0, 7)], recv_sem.at[5])

    def sum_a(i, _):
        y = lax.rem(cy + i, 4)
        for z in range(4):
            send_a2[y, z] = gathered(codes_a, recv_a, z * 4 + y)
        remote(send_a2.at[y], recv_a2.at[cy], 8, at_y(y))
        return 0

    lax.fori_loop(1, 4, sum_a, 0)
    for z in range(4):
        recv_a2[cy, z] = gathered(codes_a, recv_a, z * 4 + cy)
    finish(recv_b.at[:, pl.ds(0, 7)], recv_sem.at[4])

    @pl.when(starts)
    def _():
        finish(own, recv_sem.at[15])
        remote(wrapped, before, 16, above)

    @pl.when(ends)
    def _():
        finish(own, recv_sem.at[15])
        remote(wrapped, after, 16, below)


    def sum_b(i, _):
        x = lax.rem(cx + i, 4)
        for y in range(4):
            send_b2[x, y] = gathered(codes_b, recv_b, x * 4 + y)
        remote(send_b2.at[x], recv_b2.at[cx], 9, at_x(x))
        return 0

    lax.fori_loop(1, 4, sum_b, 0)
    for y in range(4):
        recv_b2[cx, y] = gathered(codes_b, recv_b, cx * 4 + y)

    finish(tiles_hi.at[pl.ds(0, 9)], recv_sem.at[14])
    for x in range(4):
        half = tiles_hi.at[pl.ds((x * 2 + cc) * 4, 4)]
        remote(half, half, 11, sibling)

    finish(tiles_hi.at[pl.ds(0, 16)], recv_sem.at[11])

    def merge(t):
        halves = []
        for h in range(2):
            tile = 2 * t + h
            wh, wl = split(tops[pl.ds(tile * 2 * K, 2 * K), :])
            halves.append((tiles_hi[tile], wh, wl, tile))
        return halves

    def keep(t, merged):
        hi, lo = split(jnp.concatenate(merged, axis=1))
        tiles_hi[32 + t] = hi
        tiles_lo[t] = lo
        return 0

    def merge_first(t, _):
        return keep(t, [mm(a, wh) + mm(a, wl) for a, wh, wl, _ in merge(t)])

    def merge_next(t, _):
        return keep(t, [
            mm(a, wh) + (mm(a, wl) + mm(tiles_lo[tile - 32], wh)) for a, wh, wl, tile in merge(t)
        ])

    for t in range(31):
        if t < 16:
            merge_first(t, 0)
        else:
            merge_next(t, 0)

    def summed(recv, place):
        total = recv[0, place].astype(F32)
        for s in range(1, 4):
            total += recv[s, place].astype(F32)
        return total.astype(BF)

    finish(recv_a2.at[pl.ds(0, 3)], recv_sem.at[8])
    for z in others(cz, 4):
        send_a3[z] = summed(recv_a2, z)
        remote(send_a3.at[z], recv_a3.at[cz], 12, at_z(z))
    recv_a3[cz] = summed(recv_a2, cz)
    finish(recv_b2.at[pl.ds(0, 3)], recv_sem.at[9])
    for y in others(cy, 4):
        send_b3[y] = summed(recv_b2, y)
        remote(send_b3.at[y], recv_b3.at[cy], 13, at_y(y))
    recv_b3[cy] = summed(recv_b2, cy)

    fars = []
    for m in range(6):
        total = None
        for j in range(FAR_TOP):
            partner = part_sm[j, rows_up[m]]
            tile = tiles_hi[64 - (64 >> m) + lax.div(partner, 2)].astype(F32)
            side = jnp.full((R, K), lax.rem(partner, 2), jnp.int32)
            picked = jnp.where(side == 0, tile[:, :K], tile[:, K:])
            term = mm(picked.astype(BF), block(35 + m * FAR_TOP + j).astype(BF))
            total = term if total is None else total + term
        fars.append(total)
    answer = fars[5]
    for m in range(4, -1, -1):
        answer = fars[m] + precise(answer, block(30 + m))
    answers = [precise(answer, block(15 + 6))]
    for count in (2, 4):
        start = 15 + LEAF_DEV - 2 * count
        answers = [precise(answers[i // 2], block(start + i)) for i in range(count)]
    for l in range(LEAF_DEV):
        tree_leaf[l] = precise(answers[l // 2], block(22 + l)).T

    @pl.when(cy > 0)
    def _():
        finish(own, recv_sem.at[0])

    @pl.when(cy < 3)
    def _():
        finish(own, recv_sem.at[1])

    @pl.when(jnp.logical_or(starts, ends))
    def _():
        finish(own, recv_sem.at[16])

    for l in range(LEAF_DEV):
        total = near_acc[:, l * P_SIZE:(l + 1) * P_SIZE]
        for j in range(1, NEAR):
            at = near_sm[j, l] - (me * LEAF_DEV - LEAF_DEV)
            source = rhs3[jnp.minimum(jnp.maximum(at, 0), 3 * LEAF_DEV - 1)]
            total += mm(source, nearv[j, :, l * P_SIZE:(l + 1) * P_SIZE])
        near_acc[:, l * P_SIZE:(l + 1) * P_SIZE] = total

    got_row.wait()
    finish(recv_a3.at[pl.ds(0, 3)], recv_sem.at[12])
    finish(recv_b3.at[pl.ds(0, 3)], recv_sem.at[13])
    for l in range(LEAF_DEV):
        rows = slice(l * HALF, (l + 1) * HALF)
        upper = recv_a3[0, rows, :].astype(F32)
        lower = recv_b3[0, rows, :].astype(F32)
        for s in range(1, 4):
            upper += recv_a3[s, rows, :].astype(F32)
            lower += recv_b3[s, rows, :].astype(F32)
        answer_low = (jnp.concatenate([upper, lower], axis=0) + tree_leaf[l]).astype(BF)
        far = lax.dot_general(answer_low, part(rowv, l), tn, preferred_element_type=F32)
        out[:, l * P_SIZE:(l + 1) * P_SIZE] = (far + part(near_acc, l)).astype(BF)

    @pl.when(cy < 3)
    def _():
        finish(own, send_sem.at[0])

    @pl.when(cy > 0)
    def _():
        finish(own, send_sem.at[1])

    @pl.when(jnp.logical_or(starts, ends))
    def _():
        finish(own, send_sem.at[15])
        finish(own, send_sem.at[16])

    finish(meta_a.at[pl.ds(0, 7)], send_sem.at[2])
    finish(meta_b.at[pl.ds(0, 7)], send_sem.at[3])
    finish(send_b.at[pl.ds(0, 7)], send_sem.at[4])
    finish(send_a.at[pl.ds(0, 7)], send_sem.at[5])
    finish(roots.at[pl.ds(0, 3)], send_sem.at[6])
    finish(tiles_hi.at[pl.ds(0, 3)], send_sem.at[7])
    finish(send_a2.at[pl.ds(0, 3)], send_sem.at[8])
    finish(send_b2.at[pl.ds(0, 3)], send_sem.at[9])
    finish(tiles_hi.at[pl.ds(0, 3)], send_sem.at[10])
    finish(tiles_hi.at[pl.ds(0, 9)], send_sem.at[14])
    finish(tiles_hi.at[pl.ds(0, 16)], send_sem.at[11])
    finish(send_a3.at[pl.ds(0, 3)], send_sem.at[12])
    finish(send_b3.at[pl.ds(0, 3)], send_sem.at[13])


def body(
    rhs, col_basis, row_basis, near_blocks, near_list, leaf_up, leaf_down, local_up, local_down,
    leaf_coupling, leaf_target, leaf_slot, top_up, top_down, upper_coupling, upper_partners,
):
    smem = pl.BlockSpec(memory_space=pltpu.SMEM)
    vmem = pl.BlockSpec(memory_space=pltpu.VMEM)
    hbm = pl.BlockSpec(memory_space=pl.ANY)
    width = LEAF_DEV * P_SIZE
    leaf_rows = LEAF_DEV * HALF
    return pl.pallas_call(
        kernel,
        out_shape=jax.ShapeDtypeStruct((R, width), BF),
        in_specs=[smem] * 2 + [vmem] * 8 + [hbm] * 6,
        out_specs=vmem,
        scratch_shapes=[
            pltpu.VMEM((3 * LEAF_DEV, R, P_SIZE), BF),
            pltpu.VMEM((LEAF_DEV, R, P_SIZE), BF),
            pltpu.VMEM((NEAR, P_SIZE, width), BF),
            pltpu.VMEM((LEAF_DEV, K, FAR_LEAF * K), BF),
            pltpu.VMEM((K, width), BF),
            pltpu.VMEM((D - 4, K * K), F32),
            pltpu.VMEM((D - 4, K * K), F32),
            pltpu.VMEM((6, FAR_TOP, K * K), BF),
            pltpu.VMEM((8, D), jnp.int32),
            pltpu.SMEM((8, D), jnp.int32),
            pltpu.VMEM((D, D), jnp.int32),
            pltpu.VMEM((8, NY, D), jnp.int32),
            pltpu.VMEM((LEAF_DEV * FAR_LEAF, K, R), BF),
            pltpu.VMEM((8, NY, K, R), BF),
            pltpu.VMEM((NY, 8, K, R), BF),
            pltpu.VMEM((8, NY, K, R), BF),
            pltpu.VMEM((NY, 8, K, R), BF),
            pltpu.VMEM((8, NY, D), jnp.int32),
            pltpu.VMEM((8, NY, D), jnp.int32),
            pltpu.VMEM((NY, 8 * K), jnp.int32),
            pltpu.VMEM((NY, 8 * K), jnp.int32),
            pltpu.VMEM((4, 4, leaf_rows, R), BF),
            pltpu.VMEM((4, 4, leaf_rows, R), BF),
            pltpu.VMEM((4, 4, leaf_rows, R), BF),
            pltpu.VMEM((4, 4, leaf_rows, R), BF),
            pltpu.VMEM((4, leaf_rows, R), BF),
            pltpu.VMEM((4, leaf_rows, R), BF),
            pltpu.VMEM((4, leaf_rows, R), BF),
            pltpu.VMEM((4, leaf_rows, R), BF),
            pltpu.VMEM((4, R, 2 * K), BF),
            pltpu.VMEM((63, R, 2 * K), BF),
            pltpu.VMEM((31, R, 2 * K), BF),
            pltpu.VMEM(((D - 4) * K, K), F32),
            pltpu.VMEM((59 * K, K), F32),
            pltpu.VMEM((R, width), F32),
            pltpu.VMEM((LEAF_DEV, K, R), F32),
            pltpu.SemaphoreType.DMA((12,)),
            pltpu.SemaphoreType.DMA((17,)),
            pltpu.SemaphoreType.DMA((17,)),
        ],
        compiler_params=pltpu.CompilerParams(
            collective_id=0, has_side_effects=True, vmem_limit_bytes=60 * 1024 * 1024
        ),
    )(
        near_list.T, upper_partners.T,
        rhs, col_basis, leaf_up, leaf_down, local_up, local_down, leaf_target, leaf_slot,
        row_basis, near_blocks, leaf_coupling, top_up, top_down, upper_coupling,
    )


def solution(mesh):
    flat = ("gx", "gy")
    placed = (
        P(None, flat), P(None, flat), P(None, flat), P(None, None, flat),
        P(flat, None), P(flat, None), P(flat, None), P(flat, None), P(flat, None),
        P(flat, None, None), P(flat, None), P(flat, None),
        P(), P(), P(), P(),
    )
    return jax.shard_map(body, mesh=mesh, in_specs=placed, out_specs=P(None, flat), check_vma=False)
```

```python
import jax
import jax.numpy as jnp
from jax import lax
from jax.experimental import pallas as pl
from jax.experimental.pallas import tpu as pltpu
from jax.sharding import PartitionSpec as P

K = 64
R = 128
P_SIZE = 256
LEAF_DEV = 8
NEAR = 4
FAR_LEAF = 16
FAR_TOP = 4
NX = 8
NY = 16
D = NX * NY
HALF = K // 2
MESH = pl.DeviceIdType.MESH
BF = jnp.bfloat16
F32 = jnp.float32


def mm(a, b):
    return jnp.dot(a, b, preferred_element_type=F32)


def split(x):
    hi = x.astype(BF)
    return hi, (x - hi.astype(F32)).astype(BF)


def precise(a, w):
    a_hi, a_lo = split(a)
    w_hi, w_lo = split(w)
    return mm(a_hi, w_hi) + (mm(a_lo, w_hi) + mm(a_hi, w_lo))


def unroll(rows, count, squares, first):
    for q in range(K // 2):
        pair = rows[:, q * 2 * K:(q + 1) * 2 * K].astype(F32)
        for h in range(2):
            at = first * K + 2 * q + h
            squares[pl.ds(at, count, stride=K), :] = pair[:, h * K:(h + 1) * K]


def kernel(
    near_sm, part_sm,
    rhs, col, leaf_up, leaf_down, local_up, local_down, target, slot,
    row_hbm, near_hbm, coup_hbm, tup_hbm, tdn_hbm, ucp_hbm,
    out,
    rhs3, wrapped, nearv, coupv, rowv, tupv, tdnv, ucpv,
    table, table_sm, code, code_b,
    prods, send_a, recv_a, send_b, recv_b, meta_a, meta_b, codes_a, codes_b,
    send_a2, recv_a2, send_b2, recv_b2, send_a3, recv_a3, send_b3, recv_b3,
    roots, tiles_hi, tiles_lo, tops, squares, near_acc, tree_leaf,
    local_sem, send_sem, recv_sem,
):
    mx = lax.axis_index("gx")
    my = lax.axis_index("gy")
    me = mx * NY + my
    cx, cc = lax.div(mx, 2), lax.rem(mx, 2)
    cz, cy = lax.div(my, 4), lax.rem(my, 4)
    zc = cz * 2 + cc

    def at_x(x):
        return (x * 2 + cc, my)

    def at_y(y):
        return (mx, cz * 4 + y)

    def at_z(z):
        return (mx, z * 4 + cy)

    def at_gx(x):
        return (x, my)

    def at_zc(g):
        return (cx * 2 + lax.rem(g, 2), lax.div(g, 2) * 4 + cy)

    sibling = (cx * 2 + 1 - cc, my)

    def fetch(src, dst, number):
        copy = pltpu.make_async_copy(src, dst, local_sem.at[number])
        copy.start()
        return copy

    def remote(src, dst, number, device):
        pltpu.make_async_remote_copy(
            src_ref=src, dst_ref=dst, send_sem=send_sem.at[number], recv_sem=recv_sem.at[number],
            device_id=device, device_id_type=MESH,
        ).start()

    def finish(ref, sem):
        pltpu.make_async_copy(ref, ref, sem).wait()

    def block(i):
        return squares[i * K:(i + 1) * K, :]

    def others(mine, count):
        return [lax.rem(mine + i, count) for i in range(1, count)]

    above = lax.rem(me + 4, D)
    below = lax.rem(me + D - 4, D)
    above = (lax.div(above, NY), lax.rem(above, NY))
    below = (lax.div(below, NY), lax.rem(below, NY))

    barrier = pltpu.get_barrier_semaphore()
    peers = [at_gx(x) for x in others(mx, NX)] + [at_zc(g) for g in others(zc, 8)]
    peers += [at_y(y) for y in others(cy, 4)] + [above, below]
    for peer in peers:
        pl.semaphore_signal(barrier, inc=1, device_id=peer, device_id_type=MESH)

    got_coup = fetch(coup_hbm, coupv, 0)
    got_near = fetch(near_hbm, nearv, 1)
    got_row = fetch(row_hbm, rowv, 2)
    got_tup = fetch(tup_hbm, tupv, 3)
    got_tdn = fetch(tdn_hbm, tdnv, 4)
    rows_up = [D - (D >> level - 1) + lax.div(me, 1 << level) for level in range(1, 7)]
    got_ucp = [fetch(ucp_hbm.at[rows_up[m]], ucpv.at[m], 5 + m) for m in range(6)]

    lane = lax.broadcasted_iota(jnp.int32, (LEAF_DEV, D), 1)
    row = lax.broadcasted_iota(jnp.int32, (LEAF_DEV, D), 0)
    named = jnp.full((LEAF_DEV, D), -1, jnp.int32)
    for j in range(FAR_LEAF):
        entry = (row * FAR_LEAF + j) * LEAF_DEV + slot[:, j:j + 1]
        named = jnp.where(target[:, j:j + 1] == lane, entry, named)
    last = jnp.max(named, axis=0, keepdims=True)
    first = jnp.min(jnp.where(named < 0, 1 << 20, named), axis=0, keepdims=True)
    first = jnp.where(last < 0, -1, first)
    last = jnp.where(last == first, -1, last)
    lists = jnp.where(row == 0, first, last)
    table[...] = lax.shift_right_logical(jnp.maximum(lists, 0), 3)
    got_table = fetch(table, table_sm, 11)

    def part(ref, l):
        return ref[:, l * P_SIZE:(l + 1) * P_SIZE]

    nt = (((1,), (1,)), ((), ()))
    tn = (((0,), (0,)), ((), ()))
    low = [
        lax.dot_general(part(col, l), part(rhs, l), nt, preferred_element_type=F32).astype(BF)
        for l in range(LEAF_DEV)
    ]
    for l in range(LEAF_DEV):
        rhs3[LEAF_DEV + l] = part(rhs, l)
    own = rhs3.at[pl.ds(LEAF_DEV, LEAF_DEV)]
    wide = lax.broadcasted_iota(jnp.int32, (D, D), 1)
    pick = jnp.where(
        (wide & HALF) == 0,
        jnp.broadcast_to(first, (D, D)).T,
        jnp.broadcast_to(last, (D, D)).T,
    )
    code[...] = jnp.where(pick < 0, -1, (pick & (LEAF_DEV - 1)) * HALF + (wide & (HALF - 1)))
    for g in range(8):
        for x in range(4):
            base = (x * 2 + g % 2) * NY + (g // 2) * 4
            code_b[g, x * 4:(x + 1) * 4, :] = code[base:base + 4, :]

    meta_a[mx] = code[pl.ds(pl.multiple_of(mx * NY, NY), NY), :]
    meta_b[zc] = code_b[zc]

    got_coup.wait()
    for l in range(LEAF_DEV):
        product = lax.dot_general(coupv[l], low[l], tn, preferred_element_type=F32)
        prods[l * FAR_LEAF:(l + 1) * FAR_LEAF] = product.astype(BF).reshape(FAR_LEAF, K, R)

    got_table.wait()
    coef = [
        lax.dot_general(part(rhs, l), part(col, l), nt, preferred_element_type=F32)
        for l in range(LEAF_DEV)
    ]
    unroll(leaf_up, 8, squares, 0)
    lifted = [precise(coef[l], block(l)) for l in range(LEAF_DEV)]
    unroll(local_up, 7, squares, 8)
    start = 8
    while len(lifted) > 1:
        coef = [lifted[2 * i] + lifted[2 * i + 1] for i in range(len(lifted) // 2)]
        lifted = [precise(coef[i], block(start + i)) for i in range(len(coef))]
        start += len(coef)
    pl.semaphore_wait(barrier, len(peers))
    roots[cy] = jnp.concatenate(split(lifted[0]), axis=1)
    for y in others(cy, 4):
        remote(roots.at[cy], roots.at[cy], 6, at_y(y))

    before = rhs3.at[pl.ds(0, LEAF_DEV)]
    after = rhs3.at[pl.ds(2 * LEAF_DEV, LEAF_DEV)]
    up, down = at_y(lax.rem(cy + 1, 4)), at_y(lax.rem(cy + 3, 4))
    starts, ends = cy == 0, cy == 3

    @pl.when(ends)
    def _():
        remote(own, wrapped, 15, up)
        remote(own, after, 1, down)

    @pl.when(starts)
    def _():
        remote(own, before, 0, up)
        remote(own, wrapped, 15, down)

    @pl.when(jnp.logical_and(cy > 0, cy < 3))
    def _():
        remote(own, before, 0, up)
        remote(own, after, 1, down)

    for x in others(mx, NX):
        remote(code.at[pl.ds(pl.multiple_of(x * NY, NY), NY)], meta_a.at[mx], 2, at_gx(x))
    for g in others(zc, 8):
        remote(code_b.at[g], meta_b.at[zc], 3, at_zc(g))

    def place_a(x):
        for g in range(NY):
            for c in range(2):
                product = prods[table_sm[c, x * NY + g]]
                send_a[x, g, c * HALF:(c + 1) * HALF, :] = product[:HALF]

    def place_b(g):
        for x in range(4):
            for y in range(4):
                device = (x * 2 + lax.rem(g, 2)) * NY + lax.div(g, 2) * 4 + y
                for c in range(2):
                    product = prods[table_sm[c, device]]
                    send_b[g, x * 4 + y, c * HALF:(c + 1) * HALF, :] = product[HALF:]

    def step_first(i, _):
        x = lax.rem(mx + i, NX)
        place_a(x)
        remote(send_a.at[x], recv_a.at[:, mx], 5, at_gx(x))
        g = lax.rem(zc + i, 8)
        place_b(g)
        remote(send_b.at[g], recv_b.at[:, zc], 4, at_zc(g))
        return 0

    lax.fori_loop(1, 3, step_first, 0)
    finish(roots.at[pl.ds(0, 3)], recv_sem.at[6])
    first_lanes = lax.broadcasted_iota(jnp.int32, (R, 2 * K), 1) < K
    r = [roots[h].astype(F32) for h in range(4)]
    r = [r[0] + r[1], r[2] + r[3]]
    r = [v + pltpu.roll(v, K, 1) for v in r]
    mine = tiles_hi.at[mx * 4 + cz]
    mine[...] = jnp.where(first_lanes, r[0], r[1]).astype(BF)
    for z in others(cz, 4):
        remote(mine, mine, 7, at_z(z))

    lax.fori_loop(3, 5, step_first, 0)
    finish(tiles_hi.at[pl.ds(0, 3)], recv_sem.at[7])
    column = tiles_hi.at[mx * 4 + cy]
    for x in others(cx, 4):
        remote(column, column, 10, at_x(x))

    lax.fori_loop(5, 7, step_first, 0)
    finish(tiles_hi.at[pl.ds(0, 3)], recv_sem.at[10])
    for x in others(cx, 4):
        column = tiles_hi.at[(x * 2 + cc) * 4 + cy]
        for y in others(cy, 4):
            remote(column, column, 14, at_y(y))
    lax.fori_loop(7, 8, step_first, 0)
    place_a(mx)
    place_b(zc)
    recv_a[:, mx] = send_a[mx]
    recv_b[:, zc] = send_b[zc]

    got_near.wait()
    for l in range(LEAF_DEV):
        near_acc[:, l * P_SIZE:(l + 1) * P_SIZE] = mm(part(rhs, l), nearv[0, :, l * P_SIZE:(l + 1) * P_SIZE])

    got_tup.wait()

    def turn(g, _):
        unroll(tupv.at[pl.ds(g * 8, 8)], 8, tops, g * 8)
        return 0

    lax.fori_loop(0, 15, turn, 0)
    unroll(tupv.at[120:124], 4, tops, 120)
    unroll(local_down, 7, squares, 15)
    unroll(leaf_down, 8, squares, 22)
    got_tdn.wait()
    for m in range(5):
        unroll(tdnv.at[pl.ds(rows_up[m], 1)], 1, squares, 30 + m)
    for m in range(6):
        got_ucp[m].wait()
        unroll(ucpv.at[m], FAR_TOP, squares, 35 + m * FAR_TOP)

    @pl.when(starts)
    def _():
        finish(own, recv_sem.at[15])
        remote(wrapped, before, 16, above)

    @pl.when(ends)
    def _():
        finish(own, recv_sem.at[15])
        remote(wrapped, after, 16, below)


    finish(meta_a.at[pl.ds(0, 7)], recv_sem.at[2])
    finish(meta_b.at[pl.ds(0, 7)], recv_sem.at[3])
    lanes = lax.broadcasted_iota(jnp.int32, (NY, 128), 1) < 2 * HALF
    for q in range(NX // 2):
        codes_a[:, q * 128:(q + 1) * 128] = jnp.where(lanes, meta_a[2 * q], meta_a[2 * q + 1])
        codes_b[:, q * 128:(q + 1) * 128] = jnp.where(lanes, meta_b[2 * q], meta_b[2 * q + 1])

    def gathered(codes, recv, g):
        width = codes.shape[1]
        rows = lax.broadcasted_iota(jnp.int32, (LEAF_DEV * HALF, width), 0)
        hits = jnp.where(rows == codes[pl.ds(g, 1), :], 1.0, 0.0).astype(BF)
        return mm(hits, recv[g].reshape(width, R)).astype(BF)

    finish(recv_a.at[:, pl.ds(0, 7)], recv_sem.at[5])

    def sum_a(i, _):
        y = lax.rem(cy + i, 4)
        for z in range(4):
            send_a2[y, z] = gathered(codes_a, recv_a, z * 4 + y)
        remote(send_a2.at[y], recv_a2.at[cy], 8, at_y(y))
        return 0

    lax.fori_loop(1, 4, sum_a, 0)
    for z in range(4):
        recv_a2[cy, z] = gathered(codes_a, recv_a, z * 4 + cy)
    finish(recv_b.at[:, pl.ds(0, 7)], recv_sem.at[4])

    def sum_b(i, _):
        x = lax.rem(cx + i, 4)
        for y in range(4):
            send_b2[x, y] = gathered(codes_b, recv_b, x * 4 + y)
        remote(send_b2.at[x], recv_b2.at[cx], 9, at_x(x))
        return 0

    lax.fori_loop(1, 4, sum_b, 0)
    for y in range(4):
        recv_b2[cx, y] = gathered(codes_b, recv_b, cx * 4 + y)

    finish(tiles_hi.at[pl.ds(0, 9)], recv_sem.at[14])
    for x in range(4):
        half = tiles_hi.at[pl.ds((x * 2 + cc) * 4, 4)]
        remote(half, half, 11, sibling)

    finish(tiles_hi.at[pl.ds(0, 16)], recv_sem.at[11])

    def merge(t):
        halves = []
        for h in range(2):
            tile = 2 * t + h
            wh, wl = split(tops[pl.ds(tile * 2 * K, 2 * K), :])
            halves.append((tiles_hi[tile], wh, wl, tile))
        return halves

    def keep(t, merged):
        hi, lo = split(jnp.concatenate(merged, axis=1))
        tiles_hi[32 + t] = hi
        tiles_lo[t] = lo
        return 0

    def merge_first(t, _):
        return keep(t, [mm(a, wh) + mm(a, wl) for a, wh, wl, _ in merge(t)])

    def merge_next(t, _):
        return keep(t, [
            mm(a, wh) + (mm(a, wl) + mm(tiles_lo[tile - 32], wh)) for a, wh, wl, tile in merge(t)
        ])

    for t in range(31):
        if t < 16:
            merge_first(t, 0)
        else:
            merge_next(t, 0)

    def summed(recv, place):
        total = recv[0, place].astype(F32)
        for s in range(1, 4):
            total += recv[s, place].astype(F32)
        return total.astype(BF)

    finish(recv_a2.at[pl.ds(0, 3)], recv_sem.at[8])
    for z in others(cz, 4):
        send_a3[z] = summed(recv_a2, z)
        remote(send_a3.at[z], recv_a3.at[cz], 12, at_z(z))
    recv_a3[cz] = summed(recv_a2, cz)
    finish(recv_b2.at[pl.ds(0, 3)], recv_sem.at[9])
    for y in others(cy, 4):
        send_b3[y] = summed(recv_b2, y)
        remote(send_b3.at[y], recv_b3.at[cy], 13, at_y(y))
    recv_b3[cy] = summed(recv_b2, cy)

    fars = []
    for m in range(6):
        total = None
        for j in range(FAR_TOP):
            partner = part_sm[j, rows_up[m]]
            tile = tiles_hi[64 - (64 >> m) + lax.div(partner, 2)].astype(F32)
            side = jnp.full((R, K), lax.rem(partner, 2), jnp.int32)
            picked = jnp.where(side == 0, tile[:, :K], tile[:, K:])
            term = mm(picked.astype(BF), block(35 + m * FAR_TOP + j).astype(BF))
            total = term if total is None else total + term
        fars.append(total)
    answer = fars[5]
    for m in range(4, -1, -1):
        answer = fars[m] + precise(answer, block(30 + m))
    answers = [precise(answer, block(15 + 6))]
    for count in (2, 4):
        start = 15 + LEAF_DEV - 2 * count
        answers = [precise(answers[i // 2], block(start + i)) for i in range(count)]
    for l in range(LEAF_DEV):
        tree_leaf[l] = precise(answers[l // 2], block(22 + l)).T

    @pl.when(cy > 0)
    def _():
        finish(own, recv_sem.at[0])

    @pl.when(cy < 3)
    def _():
        finish(own, recv_sem.at[1])

    @pl.when(jnp.logical_or(starts, ends))
    def _():
        finish(own, recv_sem.at[16])

    for l in range(LEAF_DEV):
        total = near_acc[:, l * P_SIZE:(l + 1) * P_SIZE]
        for j in range(1, NEAR):
            at = near_sm[j, l] - (me * LEAF_DEV - LEAF_DEV)
            source = rhs3[jnp.minimum(jnp.maximum(at, 0), 3 * LEAF_DEV - 1)]
            total += mm(source, nearv[j, :, l * P_SIZE:(l + 1) * P_SIZE])
        near_acc[:, l * P_SIZE:(l + 1) * P_SIZE] = total

    got_row.wait()
    finish(recv_a3.at[pl.ds(0, 3)], recv_sem.at[12])
    finish(recv_b3.at[pl.ds(0, 3)], recv_sem.at[13])
    for l in range(LEAF_DEV):
        rows = slice(l * HALF, (l + 1) * HALF)
        upper = recv_a3[0, rows, :].astype(F32)
        lower = recv_b3[0, rows, :].astype(F32)
        for s in range(1, 4):
            upper += recv_a3[s, rows, :].astype(F32)
            lower += recv_b3[s, rows, :].astype(F32)
        answer_low = (jnp.concatenate([upper, lower], axis=0) + tree_leaf[l]).astype(BF)
        far = lax.dot_general(answer_low, part(rowv, l), tn, preferred_element_type=F32)
        out[:, l * P_SIZE:(l + 1) * P_SIZE] = (far + part(near_acc, l)).astype(BF)

    @pl.when(cy < 3)
    def _():
        finish(own, send_sem.at[0])

    @pl.when(cy > 0)
    def _():
        finish(own, send_sem.at[1])

    @pl.when(jnp.logical_or(starts, ends))
    def _():
        finish(own, send_sem.at[15])
        finish(own, send_sem.at[16])

    finish(meta_a.at[pl.ds(0, 7)], send_sem.at[2])
    finish(meta_b.at[pl.ds(0, 7)], send_sem.at[3])
    finish(send_b.at[pl.ds(0, 7)], send_sem.at[4])
    finish(send_a.at[pl.ds(0, 7)], send_sem.at[5])
    finish(roots.at[pl.ds(0, 3)], send_sem.at[6])
    finish(tiles_hi.at[pl.ds(0, 3)], send_sem.at[7])
    finish(send_a2.at[pl.ds(0, 3)], send_sem.at[8])
    finish(send_b2.at[pl.ds(0, 3)], send_sem.at[9])
    finish(tiles_hi.at[pl.ds(0, 3)], send_sem.at[10])
    finish(tiles_hi.at[pl.ds(0, 9)], send_sem.at[14])
    finish(tiles_hi.at[pl.ds(0, 16)], send_sem.at[11])
    finish(send_a3.at[pl.ds(0, 3)], send_sem.at[12])
    finish(send_b3.at[pl.ds(0, 3)], send_sem.at[13])


def body(
    rhs, col_basis, row_basis, near_blocks, near_list, leaf_up, leaf_down, local_up, local_down,
    leaf_coupling, leaf_target, leaf_slot, top_up, top_down, upper_coupling, upper_partners,
):
    smem = pl.BlockSpec(memory_space=pltpu.SMEM)
    vmem = pl.BlockSpec(memory_space=pltpu.VMEM)
    hbm = pl.BlockSpec(memory_space=pl.ANY)
    width = LEAF_DEV * P_SIZE
    leaf_rows = LEAF_DEV * HALF
    return pl.pallas_call(
        kernel,
        out_shape=jax.ShapeDtypeStruct((R, width), BF),
        in_specs=[smem] * 2 + [vmem] * 8 + [hbm] * 6,
        out_specs=vmem,
        scratch_shapes=[
            pltpu.VMEM((3 * LEAF_DEV, R, P_SIZE), BF),
            pltpu.VMEM((LEAF_DEV, R, P_SIZE), BF),
            pltpu.VMEM((NEAR, P_SIZE, width), BF),
            pltpu.VMEM((LEAF_DEV, K, FAR_LEAF * K), BF),
            pltpu.VMEM((K, width), BF),
            pltpu.VMEM((D - 4, K * K), F32),
            pltpu.VMEM((D - 4, K * K), F32),
            pltpu.VMEM((6, FAR_TOP, K * K), BF),
            pltpu.VMEM((8, D), jnp.int32),
            pltpu.SMEM((8, D), jnp.int32),
            pltpu.VMEM((D, D), jnp.int32),
            pltpu.VMEM((8, NY, D), jnp.int32),
            pltpu.VMEM((LEAF_DEV * FAR_LEAF, K, R), BF),
            pltpu.VMEM((8, NY, K, R), BF),
            pltpu.VMEM((NY, 8, K, R), BF),
            pltpu.VMEM((8, NY, K, R), BF),
            pltpu.VMEM((NY, 8, K, R), BF),
            pltpu.VMEM((8, NY, D), jnp.int32),
            pltpu.VMEM((8, NY, D), jnp.int32),
            pltpu.VMEM((NY, 8 * K), jnp.int32),
            pltpu.VMEM((NY, 8 * K), jnp.int32),
            pltpu.VMEM((4, 4, leaf_rows, R), BF),
            pltpu.VMEM((4, 4, leaf_rows, R), BF),
            pltpu.VMEM((4, 4, leaf_rows, R), BF),
            pltpu.VMEM((4, 4, leaf_rows, R), BF),
            pltpu.VMEM((4, leaf_rows, R), BF),
            pltpu.VMEM((4, leaf_rows, R), BF),
            pltpu.VMEM((4, leaf_rows, R), BF),
            pltpu.VMEM((4, leaf_rows, R), BF),
            pltpu.VMEM((4, R, 2 * K), BF),
            pltpu.VMEM((63, R, 2 * K), BF),
            pltpu.VMEM((31, R, 2 * K), BF),
            pltpu.VMEM(((D - 4) * K, K), F32),
            pltpu.VMEM((59 * K, K), F32),
            pltpu.VMEM((R, width), F32),
            pltpu.VMEM((LEAF_DEV, K, R), F32),
            pltpu.SemaphoreType.DMA((12,)),
            pltpu.SemaphoreType.DMA((17,)),
            pltpu.SemaphoreType.DMA((17,)),
        ],
        compiler_params=pltpu.CompilerParams(
            collective_id=0, has_side_effects=True, vmem_limit_bytes=60 * 1024 * 1024
        ),
    )(
        near_list.T, upper_partners.T,
        rhs, col_basis, leaf_up, leaf_down, local_up, local_down, leaf_target, leaf_slot,
        row_basis, near_blocks, leaf_coupling, top_up, top_down, upper_coupling,
    )


def solution(mesh):
    flat = ("gx", "gy")
    placed = (
        P(None, flat), P(None, flat), P(None, flat), P(None, None, flat),
        P(flat, None), P(flat, None), P(flat, None), P(flat, None), P(flat, None),
        P(flat, None, None), P(flat, None), P(flat, None),
        P(), P(), P(), P(),
    )
    return jax.shard_map(body, mesh=mesh, in_specs=placed, out_specs=P(None, flat), check_vma=False)
```

```python
import jax
import jax.numpy as jnp
from jax import lax
from jax.experimental import pallas as pl
from jax.experimental.pallas import tpu as pltpu
from jax.sharding import PartitionSpec as P

K = 64
R = 128
P_SIZE = 256
LEAF_DEV = 8
NEAR = 4
FAR_LEAF = 16
FAR_TOP = 4
NX = 8
NY = 16
D = NX * NY
HALF = K // 2
MESH = pl.DeviceIdType.MESH
BF = jnp.bfloat16
F32 = jnp.float32


def mm(a, b):
    return jnp.dot(a, b, preferred_element_type=F32)


def split(x):
    hi = x.astype(BF)
    return hi, (x - hi.astype(F32)).astype(BF)


def precise(a, w):
    a_hi, a_lo = split(a)
    w_hi, w_lo = split(w)
    return mm(a_hi, w_hi) + (mm(a_lo, w_hi) + mm(a_hi, w_lo))


def unroll(rows, count, squares, first):
    for q in range(K // 2):
        pair = rows[:, q * 2 * K:(q + 1) * 2 * K].astype(F32)
        for h in range(2):
            at = first * K + 2 * q + h
            squares[pl.ds(at, count, stride=K), :] = pair[:, h * K:(h + 1) * K]


def kernel(
    near_sm, part_sm,
    rhs, col, leaf_up, leaf_down, local_up, local_down, target, slot,
    row_hbm, near_hbm, coup_hbm, tup_hbm, tdn_hbm, ucp_hbm,
    out,
    rhs3, wrapped, nearv, coupv, rowv, tupv, tdnv, ucpv,
    table, table_sm, code, code_b,
    prods, send_a, recv_a, send_b, recv_b, meta_a, meta_b, codes_a, codes_b,
    send_a2, recv_a2, send_b2, recv_b2, send_a3, recv_a3, send_b3, recv_b3,
    roots, tiles_hi, tiles_lo, tops, squares, near_acc, tree_leaf,
    local_sem, send_sem, recv_sem,
):
    mx = lax.axis_index("gx")
    my = lax.axis_index("gy")
    me = mx * NY + my
    cx, cc = lax.div(mx, 2), lax.rem(mx, 2)
    cz, cy = lax.div(my, 4), lax.rem(my, 4)
    zc = cz * 2 + cc

    def at_x(x):
        return (x * 2 + cc, my)

    def at_y(y):
        return (mx, cz * 4 + y)

    def at_z(z):
        return (mx, z * 4 + cy)

    def at_gx(x):
        return (x, my)

    def at_zc(g):
        return (cx * 2 + lax.rem(g, 2), lax.div(g, 2) * 4 + cy)

    sibling = (cx * 2 + 1 - cc, my)

    def fetch(src, dst, number):
        copy = pltpu.make_async_copy(src, dst, local_sem.at[number])
        copy.start()
        return copy

    def remote(src, dst, number, device):
        pltpu.make_async_remote_copy(
            src_ref=src, dst_ref=dst, send_sem=send_sem.at[number], recv_sem=recv_sem.at[number],
            device_id=device, device_id_type=MESH,
        ).start()

    def finish(ref, sem):
        pltpu.make_async_copy(ref, ref, sem).wait()

    def block(i):
        return squares[i * K:(i + 1) * K, :]

    def others(mine, count):
        return [lax.rem(mine + i, count) for i in range(1, count)]

    above = lax.rem(me + 4, D)
    below = lax.rem(me + D - 4, D)
    above = (lax.div(above, NY), lax.rem(above, NY))
    below = (lax.div(below, NY), lax.rem(below, NY))

    barrier = pltpu.get_barrier_semaphore()
    peers = [at_gx(x) for x in others(mx, NX)] + [at_zc(g) for g in others(zc, 8)]
    peers += [at_y(y) for y in others(cy, 4)] + [above, below]
    for peer in peers:
        pl.semaphore_signal(barrier, inc=1, device_id=peer, device_id_type=MESH)

    got_coup = fetch(coup_hbm, coupv, 0)
    got_near = fetch(near_hbm, nearv, 1)
    got_row = fetch(row_hbm, rowv, 2)
    got_tup = fetch(tup_hbm, tupv, 3)
    got_tdn = fetch(tdn_hbm, tdnv, 4)
    rows_up = [D - (D >> level - 1) + lax.div(me, 1 << level) for level in range(1, 7)]
    got_ucp = [fetch(ucp_hbm.at[rows_up[m]], ucpv.at[m], 5 + m) for m in range(6)]

    lane = lax.broadcasted_iota(jnp.int32, (LEAF_DEV, D), 1)
    row = lax.broadcasted_iota(jnp.int32, (LEAF_DEV, D), 0)
    named = jnp.full((LEAF_DEV, D), -1, jnp.int32)
    for j in range(FAR_LEAF):
        entry = (row * FAR_LEAF + j) * LEAF_DEV + slot[:, j:j + 1]
        named = jnp.where(target[:, j:j + 1] == lane, entry, named)
    last = jnp.max(named, axis=0, keepdims=True)
    first = jnp.min(jnp.where(named < 0, 1 << 20, named), axis=0, keepdims=True)
    first = jnp.where(last < 0, -1, first)
    last = jnp.where(last == first, -1, last)
    lists = jnp.where(row == 0, first, last)
    table[...] = lax.shift_right_logical(jnp.maximum(lists, 0), 3)
    got_table = fetch(table, table_sm, 11)

    def part(ref, l):
        return ref[:, l * P_SIZE:(l + 1) * P_SIZE]

    nt = (((1,), (1,)), ((), ()))
    tn = (((0,), (0,)), ((), ()))
    low = [
        lax.dot_general(part(col, l), part(rhs, l), nt, preferred_element_type=F32).astype(BF)
        for l in range(LEAF_DEV)
    ]
    for l in range(LEAF_DEV):
        rhs3[LEAF_DEV + l] = part(rhs, l)
    own = rhs3.at[pl.ds(LEAF_DEV, LEAF_DEV)]
    wide = lax.broadcasted_iota(jnp.int32, (D, D), 1)
    pick = jnp.where(
        (wide & HALF) == 0,
        jnp.broadcast_to(first, (D, D)).T,
        jnp.broadcast_to(last, (D, D)).T,
    )
    code[...] = jnp.where(pick < 0, -1, (pick & (LEAF_DEV - 1)) * HALF + (wide & (HALF - 1)))
    for g in range(8):
        for x in range(4):
            base = (x * 2 + g % 2) * NY + (g // 2) * 4
            code_b[g, x * 4:(x + 1) * 4, :] = code[base:base + 4, :]

    meta_a[mx] = code[pl.ds(pl.multiple_of(mx * NY, NY), NY), :]
    meta_b[zc] = code_b[zc]

    got_coup.wait()
    for l in range(LEAF_DEV):
        product = lax.dot_general(coupv[l], low[l], tn, preferred_element_type=F32)
        prods[l * FAR_LEAF:(l + 1) * FAR_LEAF] = product.astype(BF).reshape(FAR_LEAF, K, R)

    got_table.wait()
    coef = [
        lax.dot_general(part(rhs, l), part(col, l), nt, preferred_element_type=F32)
        for l in range(LEAF_DEV)
    ]
    unroll(leaf_up, 8, squares, 0)
    lifted = [precise(coef[l], block(l)) for l in range(LEAF_DEV)]
    unroll(local_up, 7, squares, 8)
    start = 8
    while len(lifted) > 1:
        coef = [lifted[2 * i] + lifted[2 * i + 1] for i in range(len(lifted) // 2)]
        lifted = [precise(coef[i], block(start + i)) for i in range(len(coef))]
        start += len(coef)
    pl.semaphore_wait(barrier, len(peers))
    roots[cy] = jnp.concatenate(split(lifted[0]), axis=1)
    for y in others(cy, 4):
        remote(roots.at[cy], roots.at[cy], 6, at_y(y))

    before = rhs3.at[pl.ds(0, LEAF_DEV)]
    after = rhs3.at[pl.ds(2 * LEAF_DEV, LEAF_DEV)]
    up, down = at_y(lax.rem(cy + 1, 4)), at_y(lax.rem(cy + 3, 4))
    starts, ends = cy == 0, cy == 3

    @pl.when(ends)
    def _():
        remote(own, wrapped, 15, up)
        remote(own, after, 1, down)

    @pl.when(starts)
    def _():
        remote(own, before, 0, up)
        remote(own, wrapped, 15, down)

    @pl.when(jnp.logical_and(cy > 0, cy < 3))
    def _():
        remote(own, before, 0, up)
        remote(own, after, 1, down)

    for x in others(mx, NX):
        remote(code.at[pl.ds(pl.multiple_of(x * NY, NY), NY)], meta_a.at[mx], 2, at_gx(x))
    for g in others(zc, 8):
        remote(code_b.at[g], meta_b.at[zc], 3, at_zc(g))

    def place_a(x):
        for g in range(NY):
            for c in range(2):
                product = prods[table_sm[c, x * NY + g]]
                send_a[x, g, c * HALF:(c + 1) * HALF, :] = product[:HALF]

    def place_b(g):
        for x in range(4):
            for y in range(4):
                device = (x * 2 + lax.rem(g, 2)) * NY + lax.div(g, 2) * 4 + y
                for c in range(2):
                    product = prods[table_sm[c, device]]
                    send_b[g, x * 4 + y, c * HALF:(c + 1) * HALF, :] = product[HALF:]

    def step_first(i, _):
        x = lax.rem(mx + i, NX)
        place_a(x)
        remote(send_a.at[x], recv_a.at[:, mx], 5, at_gx(x))
        g = lax.rem(zc + i, 8)
        place_b(g)
        remote(send_b.at[g], recv_b.at[:, zc], 4, at_zc(g))
        return 0

    lax.fori_loop(1, 4, step_first, 0)
    finish(roots.at[pl.ds(0, 3)], recv_sem.at[6])
    first_lanes = lax.broadcasted_iota(jnp.int32, (R, 2 * K), 1) < K
    r = [roots[h].astype(F32) for h in range(4)]
    r = [r[0] + r[1], r[2] + r[3]]
    r = [v + pltpu.roll(v, K, 1) for v in r]
    mine = tiles_hi.at[mx * 4 + cz]
    mine[...] = jnp.where(first_lanes, r[0], r[1]).astype(BF)
    for z in others(cz, 4):
        remote(mine, mine, 7, at_z(z))

    lax.fori_loop(4, 7, step_first, 0)
    finish(tiles_hi.at[pl.ds(0, 3)], recv_sem.at[7])
    column = tiles_hi.at[mx * 4 + cy]
    for x in others(cx, 4):
        remote(column, column, 10, at_x(x))

    lax.fori_loop(7, 8, step_first, 0)
    finish(tiles_hi.at[pl.ds(0, 3)], recv_sem.at[10])
    for x in others(cx, 4):
        column = tiles_hi.at[(x * 2 + cc) * 4 + cy]
        for y in others(cy, 4):
            remote(column, column, 14, at_y(y))
    place_a(mx)
    place_b(zc)
    recv_a[:, mx] = send_a[mx]
    recv_b[:, zc] = send_b[zc]

    got_near.wait()
    for l in range(LEAF_DEV):
        near_acc[:, l * P_SIZE:(l + 1) * P_SIZE] = mm(part(rhs, l), nearv[0, :, l * P_SIZE:(l + 1) * P_SIZE])

    got_tup.wait()

    def turn(g, _):
        unroll(tupv.at[pl.ds(g * 8, 8)], 8, tops, g * 8)
        return 0

    lax.fori_loop(0, 15, turn, 0)
    unroll(tupv.at[120:124], 4, tops, 120)
    unroll(local_down, 7, squares, 15)
    unroll(leaf_down, 8, squares, 22)
    got_tdn.wait()
    for m in range(5):
        unroll(tdnv.at[pl.ds(rows_up[m], 1)], 1, squares, 30 + m)
    for m in range(6):
        got_ucp[m].wait()
        unroll(ucpv.at[m], FAR_TOP, squares, 35 + m * FAR_TOP)

    @pl.when(starts)
    def _():
        finish(own, recv_sem.at[15])
        remote(wrapped, before, 16, above)

    @pl.when(ends)
    def _():
        finish(own, recv_sem.at[15])
        remote(wrapped, after, 16, below)


    finish(meta_a.at[pl.ds(0, 7)], recv_sem.at[2])
    finish(meta_b.at[pl.ds(0, 7)], recv_sem.at[3])
    lanes = lax.broadcasted_iota(jnp.int32, (NY, 128), 1) < 2 * HALF
    for q in range(NX // 2):
        codes_a[:, q * 128:(q + 1) * 128] = jnp.where(lanes, meta_a[2 * q], meta_a[2 * q + 1])
        codes_b[:, q * 128:(q + 1) * 128] = jnp.where(lanes, meta_b[2 * q], meta_b[2 * q + 1])

    def gathered(codes, recv, g):
        width = codes.shape[1]
        rows = lax.broadcasted_iota(jnp.int32, (LEAF_DEV * HALF, width), 0)
        hits = jnp.where(rows == codes[pl.ds(g, 1), :], 1.0, 0.0).astype(BF)
        return mm(hits, recv[g].reshape(width, R)).astype(BF)

    finish(recv_a.at[:, pl.ds(0, 7)], recv_sem.at[5])

    def sum_a(i, _):
        y = lax.rem(cy + i, 4)
        for z in range(4):
            send_a2[y, z] = gathered(codes_a, recv_a, z * 4 + y)
        remote(send_a2.at[y], recv_a2.at[cy], 8, at_y(y))
        return 0

    lax.fori_loop(1, 4, sum_a, 0)
    for z in range(4):
        recv_a2[cy, z] = gathered(codes_a, recv_a, z * 4 + cy)
    finish(recv_b.at[:, pl.ds(0, 7)], recv_sem.at[4])

    def sum_b(i, _):
        x = lax.rem(cx + i, 4)
        for y in range(4):
            send_b2[x, y] = gathered(codes_b, recv_b, x * 4 + y)
        remote(send_b2.at[x], recv_b2.at[cx], 9, at_x(x))
        return 0

    lax.fori_loop(1, 4, sum_b, 0)
    for y in range(4):
        recv_b2[cx, y] = gathered(codes_b, recv_b, cx * 4 + y)

    finish(tiles_hi.at[pl.ds(0, 9)], recv_sem.at[14])
    for x in range(4):
        half = tiles_hi.at[pl.ds((x * 2 + cc) * 4, 4)]
        remote(half, half, 11, sibling)

    finish(tiles_hi.at[pl.ds(0, 16)], recv_sem.at[11])

    def merge(t):
        halves = []
        for h in range(2):
            tile = 2 * t + h
            wh, wl = split(tops[pl.ds(tile * 2 * K, 2 * K), :])
            halves.append((tiles_hi[tile], wh, wl, tile))
        return halves

    def keep(t, merged):
        hi, lo = split(jnp.concatenate(merged, axis=1))
        tiles_hi[32 + t] = hi
        tiles_lo[t] = lo
        return 0

    def merge_first(t, _):
        return keep(t, [mm(a, wh) + mm(a, wl) for a, wh, wl, _ in merge(t)])

    def merge_next(t, _):
        return keep(t, [
            mm(a, wh) + (mm(a, wl) + mm(tiles_lo[tile - 32], wh)) for a, wh, wl, tile in merge(t)
        ])

    for t in range(31):
        if t < 16:
            merge_first(t, 0)
        else:
            merge_next(t, 0)

    def summed(recv, place):
        total = recv[0, place].astype(F32)
        for s in range(1, 4):
            total += recv[s, place].astype(F32)
        return total.astype(BF)

    finish(recv_a2.at[pl.ds(0, 3)], recv_sem.at[8])
    for z in others(cz, 4):
        send_a3[z] = summed(recv_a2, z)
        remote(send_a3.at[z], recv_a3.at[cz], 12, at_z(z))
    recv_a3[cz] = summed(recv_a2, cz)
    finish(recv_b2.at[pl.ds(0, 3)], recv_sem.at[9])
    for y in others(cy, 4):
        send_b3[y] = summed(recv_b2, y)
        remote(send_b3.at[y], recv_b3.at[cy], 13, at_y(y))
    recv_b3[cy] = summed(recv_b2, cy)

    fars = []
    for m in range(6):
        total = None
        for j in range(FAR_TOP):
            partner = part_sm[j, rows_up[m]]
            tile = tiles_hi[64 - (64 >> m) + lax.div(partner, 2)].astype(F32)
            side = jnp.full((R, K), lax.rem(partner, 2), jnp.int32)
            picked = jnp.where(side == 0, tile[:, :K], tile[:, K:])
            term = mm(picked.astype(BF), block(35 + m * FAR_TOP + j).astype(BF))
            total = term if total is None else total + term
        fars.append(total)
    answer = fars[5]
    for m in range(4, -1, -1):
        answer = fars[m] + precise(answer, block(30 + m))
    answers = [precise(answer, block(15 + 6))]
    for count in (2, 4):
        start = 15 + LEAF_DEV - 2 * count
        answers = [precise(answers[i // 2], block(start + i)) for i in range(count)]
    for l in range(LEAF_DEV):
        tree_leaf[l] = precise(answers[l // 2], block(22 + l)).T

    @pl.when(cy > 0)
    def _():
        finish(own, recv_sem.at[0])

    @pl.when(cy < 3)
    def _():
        finish(own, recv_sem.at[1])

    @pl.when(jnp.logical_or(starts, ends))
    def _():
        finish(own, recv_sem.at[16])

    for l in range(LEAF_DEV):
        total = near_acc[:, l * P_SIZE:(l + 1) * P_SIZE]
        for j in range(1, NEAR):
            at = near_sm[j, l] - (me * LEAF_DEV - LEAF_DEV)
            source = rhs3[jnp.minimum(jnp.maximum(at, 0), 3 * LEAF_DEV - 1)]
            total += mm(source, nearv[j, :, l * P_SIZE:(l + 1) * P_SIZE])
        near_acc[:, l * P_SIZE:(l + 1) * P_SIZE] = total

    got_row.wait()
    finish(recv_a3.at[pl.ds(0, 3)], recv_sem.at[12])
    finish(recv_b3.at[pl.ds(0, 3)], recv_sem.at[13])
    for l in range(LEAF_DEV):
        rows = slice(l * HALF, (l + 1) * HALF)
        upper = recv_a3[0, rows, :].astype(F32)
        lower = recv_b3[0, rows, :].astype(F32)
        for s in range(1, 4):
            upper += recv_a3[s, rows, :].astype(F32)
            lower += recv_b3[s, rows, :].astype(F32)
        answer_low = (jnp.concatenate([upper, lower], axis=0) + tree_leaf[l]).astype(BF)
        far = lax.dot_general(answer_low, part(rowv, l), tn, preferred_element_type=F32)
        out[:, l * P_SIZE:(l + 1) * P_SIZE] = (far + part(near_acc, l)).astype(BF)

    @pl.when(cy < 3)
    def _():
        finish(own, send_sem.at[0])

    @pl.when(cy > 0)
    def _():
        finish(own, send_sem.at[1])

    @pl.when(jnp.logical_or(starts, ends))
    def _():
        finish(own, send_sem.at[15])
        finish(own, send_sem.at[16])

    finish(meta_a.at[pl.ds(0, 7)], send_sem.at[2])
    finish(meta_b.at[pl.ds(0, 7)], send_sem.at[3])
    finish(send_b.at[pl.ds(0, 7)], send_sem.at[4])
    finish(send_a.at[pl.ds(0, 7)], send_sem.at[5])
    finish(roots.at[pl.ds(0, 3)], send_sem.at[6])
    finish(tiles_hi.at[pl.ds(0, 3)], send_sem.at[7])
    finish(send_a2.at[pl.ds(0, 3)], send_sem.at[8])
    finish(send_b2.at[pl.ds(0, 3)], send_sem.at[9])
    finish(tiles_hi.at[pl.ds(0, 3)], send_sem.at[10])
    finish(tiles_hi.at[pl.ds(0, 9)], send_sem.at[14])
    finish(tiles_hi.at[pl.ds(0, 16)], send_sem.at[11])
    finish(send_a3.at[pl.ds(0, 3)], send_sem.at[12])
    finish(send_b3.at[pl.ds(0, 3)], send_sem.at[13])


def body(
    rhs, col_basis, row_basis, near_blocks, near_list, leaf_up, leaf_down, local_up, local_down,
    leaf_coupling, leaf_target, leaf_slot, top_up, top_down, upper_coupling, upper_partners,
):
    smem = pl.BlockSpec(memory_space=pltpu.SMEM)
    vmem = pl.BlockSpec(memory_space=pltpu.VMEM)
    hbm = pl.BlockSpec(memory_space=pl.ANY)
    width = LEAF_DEV * P_SIZE
    leaf_rows = LEAF_DEV * HALF
    return pl.pallas_call(
        kernel,
        out_shape=jax.ShapeDtypeStruct((R, width), BF),
        in_specs=[smem] * 2 + [vmem] * 8 + [hbm] * 6,
        out_specs=vmem,
        scratch_shapes=[
            pltpu.VMEM((3 * LEAF_DEV, R, P_SIZE), BF),
            pltpu.VMEM((LEAF_DEV, R, P_SIZE), BF),
            pltpu.VMEM((NEAR, P_SIZE, width), BF),
            pltpu.VMEM((LEAF_DEV, K, FAR_LEAF * K), BF),
            pltpu.VMEM((K, width), BF),
            pltpu.VMEM((D - 4, K * K), F32),
            pltpu.VMEM((D - 4, K * K), F32),
            pltpu.VMEM((6, FAR_TOP, K * K), BF),
            pltpu.VMEM((8, D), jnp.int32),
            pltpu.SMEM((8, D), jnp.int32),
            pltpu.VMEM((D, D), jnp.int32),
            pltpu.VMEM((8, NY, D), jnp.int32),
            pltpu.VMEM((LEAF_DEV * FAR_LEAF, K, R), BF),
            pltpu.VMEM((8, NY, K, R), BF),
            pltpu.VMEM((NY, 8, K, R), BF),
            pltpu.VMEM((8, NY, K, R), BF),
            pltpu.VMEM((NY, 8, K, R), BF),
            pltpu.VMEM((8, NY, D), jnp.int32),
            pltpu.VMEM((8, NY, D), jnp.int32),
            pltpu.VMEM((NY, 8 * K), jnp.int32),
            pltpu.VMEM((NY, 8 * K), jnp.int32),
            pltpu.VMEM((4, 4, leaf_rows, R), BF),
            pltpu.VMEM((4, 4, leaf_rows, R), BF),
            pltpu.VMEM((4, 4, leaf_rows, R), BF),
            pltpu.VMEM((4, 4, leaf_rows, R), BF),
            pltpu.VMEM((4, leaf_rows, R), BF),
            pltpu.VMEM((4, leaf_rows, R), BF),
            pltpu.VMEM((4, leaf_rows, R), BF),
            pltpu.VMEM((4, leaf_rows, R), BF),
            pltpu.VMEM((4, R, 2 * K), BF),
            pltpu.VMEM((63, R, 2 * K), BF),
            pltpu.VMEM((31, R, 2 * K), BF),
            pltpu.VMEM(((D - 4) * K, K), F32),
            pltpu.VMEM((59 * K, K), F32),
            pltpu.VMEM((R, width), F32),
            pltpu.VMEM((LEAF_DEV, K, R), F32),
            pltpu.SemaphoreType.DMA((12,)),
            pltpu.SemaphoreType.DMA((17,)),
            pltpu.SemaphoreType.DMA((17,)),
        ],
        compiler_params=pltpu.CompilerParams(
            collective_id=0, has_side_effects=True, vmem_limit_bytes=60 * 1024 * 1024
        ),
    )(
        near_list.T, upper_partners.T,
        rhs, col_basis, leaf_up, leaf_down, local_up, local_down, leaf_target, leaf_slot,
        row_basis, near_blocks, leaf_coupling, top_up, top_down, upper_coupling,
    )


def solution(mesh):
    flat = ("gx", "gy")
    placed = (
        P(None, flat), P(None, flat), P(None, flat), P(None, None, flat),
        P(flat, None), P(flat, None), P(flat, None), P(flat, None), P(flat, None),
        P(flat, None, None), P(flat, None), P(flat, None),
        P(), P(), P(), P(),
    )
    return jax.shard_map(body, mesh=mesh, in_specs=placed, out_specs=P(None, flat), check_vma=False)
```
